128 devices in a mesh: grp: 8 (over z_lo, y), seq: 16 (over z_hi, x, core).
Axes of the slice: x: 4, y: 4, z: 4 (z_hi: 2, z_lo: 2; z = z_hi * 2 + z_lo), core: 2. Of those that a mesh axis runs over, the one named last changes fastest.
Arguments:
- qkv: bfloat16 [32, 1024, 6144], P('grp', 'seq'), may hold values from -20 to 20
- text_kv: bfloat16 [32, 256, 4096], P('grp', 'seq'), may hold values from -6 to 6
- clip_blocks: int32 [32], replicated, may hold values from 1 to 4, as said below
- text_count: int32 [32], replicated, may hold values from 1 to 256, as said below
- dest_group: int32 [32], replicated, may hold values from 0 to 7, as said below
- out_weight: bfloat16 [2048, 3072], replicated, may hold values from -0.125 to 0.125
- grad_out: bfloat16 [32, 1024, 3072], P('grp', 'seq'), may hold values from -6 to 6
Outputs:
- out: bfloat16 [32, 1024, 3072], P('grp', 'seq')
- grad_qkv: bfloat16 [32, 1024, 6144], P('grp', 'seq')
- grad_text: bfloat16 [32, 256, 4096], P('grp', 'seq')
- grad_weight: float32 [2048, 3072], P('seq', 'grp')
The draws below stay inside these ranges and needn't reach their ends.
Inputs may be any that keep to these rules, and one draw needn't show every extreme that they name: Clip c has 256 * clip_blocks[c] live video tokens at its start; some clip has all 4 blocks. Clip c has text_count[c] live text tokens at its start; some clip has all 256. Clip g * 4 + j goes to place j of group dest_group[g * 4 + j]. For a fixed j these groups all differ over g, and the 4 clips of one group go to different groups, so every group receives exactly 4 clips, one in each place.
All inputs are finite; a program needn't handle non-finite values.
Results may differ from the reference program's by a relative error of at most 0.023.
Values may be sent and summed in bfloat16 or wider, within the bound.
A program may use at most 256 MiB of HBM per device.

```python
import jax
import jax.numpy as jnp
from jax import lax

D = 3072
HEAD = 128
HEADS = 16
BLK = 256
LBLK = 4
CPG = 4
TXT = 256
HW = 2048
LCLIP = 1024
CLIPS = 32


def draw_qkv(key, part):
    key = jax.random.fold_in(key, 11)
    shape = (CLIPS, LCLIP, 3, HEADS, HEAD)
    whole = jax.random.truncated_normal(key, -6.0, 6.0, shape, jnp.float32)
    return whole.reshape(CLIPS, LCLIP, 3 * HEADS * HEAD).astype(jnp.bfloat16)


def draw_clip_blocks(key, part):
    key = jax.random.fold_in(key, 21)
    first_key, second_key = jax.random.split(key)
    blocks = jax.random.randint(first_key, (CLIPS,), 1, LBLK + 1)
    longest = jax.random.randint(second_key, (), 0, CLIPS)
    return jnp.where(jnp.arange(CLIPS) == longest, LBLK, blocks).astype(jnp.int32)


def draw_text_count(key, part):
    key = jax.random.fold_in(key, 31)
    first_key, second_key = jax.random.split(key)
    counts = jax.random.randint(first_key, (CLIPS,), 1, TXT + 1)
    longest = jax.random.randint(second_key, (), 0, CLIPS)
    return jnp.where(jnp.arange(CLIPS) == longest, TXT, counts).astype(jnp.int32)


def draw_dest_group(key, part):
    key = jax.random.fold_in(key, 41)
    first_key, second_key, third_key = jax.random.split(key, 3)
    group_total = CLIPS // CPG
    relabel = jax.random.permutation(first_key, group_total)
    rotate = jax.random.permutation(second_key, group_total)
    offsets = jax.random.permutation(third_key, group_total)[:CPG]
    table = relabel[(rotate[:, None] + offsets[None, :]) % group_total]
    return table.reshape(CLIPS).astype(jnp.int32)


def spiked(values, key, source, target, shards_of, factor):
    owner, partner = [(jnp.arange(values.shape[position]) // (values.shape[position] // shards_of)).reshape([-1 if axis == position else 1 for axis in range(values.ndim)]) for position in (source, target)]
    chosen = jax.random.permutation(key, shards_of)[partner]
    strong = (owner == chosen) | (owner == (partner + shards_of // 2) % shards_of)
    return jnp.where(strong, factor * values, values)


def block_levels(key, dims, shards, smallest, largest):
    gain, own = 1.0, jax.random.fold_in(key, 6)
    for axis_at, parts in shards:
        heights = jnp.exp(jax.random.uniform(jax.random.fold_in(own, axis_at), (parts,), jnp.float32, smallest / len(shards), largest / len(shards)))
        gain = gain * jnp.repeat(heights, dims[axis_at] // parts).reshape([-1 if axis == axis_at else 1 for axis in range(len(dims))])
    return gain


def noise(rng, shape, spread, limit, cuts=(), kind=jnp.bfloat16):
    result = spread * jax.random.normal(rng, shape, jnp.float32)
    if cuts:
        result = result * block_levels(rng, shape, cuts, -0.22, 0.18)
    return jnp.clip(result, -limit, limit).astype(kind)


def heavy_noise(key, extent, width, bound, pieces, heavy, kind=jnp.bfloat16):
    values = width * jax.random.normal(key, extent, jnp.float32)
    if pieces:
        values = values * block_levels(key, extent, pieces, -0.22, 0.18)
    return jnp.clip(spiked(values, jax.random.fold_in(key, 3), *heavy), -bound, bound).astype(kind)


def setup_inputs(seed: int = 0) -> dict:
    seeds = jax.random.split(jax.random.key(seed), 8)
    qkv = draw_qkv(jax.random.fold_in(seeds[7], 71), 0)
    text_kv = noise(seeds[1], (CLIPS, TXT, 2 * HW), 1.0, 6.0, ((0, 8), (1, 16)))
    clip_blocks = draw_clip_blocks(jax.random.fold_in(seeds[7], 71), 0)
    text_count = draw_text_count(jax.random.fold_in(seeds[7], 71), 0)
    dest_group = draw_dest_group(jax.random.fold_in(seeds[7], 71), 0)
    out_weight = noise(seeds[5], (HW, D), HW ** -0.5, 0.125)
    grad_out = heavy_noise(seeds[6], (CLIPS, LCLIP, D), 1.0, 6.0, ((0, 8), (1, 16)), (0, 2, 8, 2.0))
    return {"qkv": qkv, "text_kv": text_kv, "clip_blocks": clip_blocks, "text_count": text_count, "dest_group": dest_group, "out_weight": out_weight, "grad_out": grad_out}


NEG_FILL = -1.0e30


def attend(queries, key_rows, value_rows, live_query, live_key):
    score_scale = HEAD ** -0.5
    scores = jnp.einsum("qhe,khe->hqk", queries.astype(jnp.float32), key_rows.astype(jnp.float32)) * score_scale
    scores = jnp.where(live_key[None, None, :], scores, NEG_FILL)
    row_max = jnp.max(scores, axis=-1, keepdims=True)
    exponent = jnp.exp(scores - row_max)
    weights = exponent / jnp.sum(exponent, axis=-1, keepdims=True)
    weights_b = weights.astype(jnp.bfloat16)
    mixed = jnp.einsum("hqk,khe->qhe", weights_b.astype(jnp.float32), value_rows.astype(jnp.float32))
    mixed = mixed * live_query[:, None, None].astype(jnp.float32)
    return mixed.astype(jnp.bfloat16), weights


def attend_back(queries, key_rows, value_rows, weights, grad_mixed):
    score_scale = HEAD ** -0.5
    weights_b = weights.astype(jnp.bfloat16).astype(jnp.float32)
    grad_f = grad_mixed.astype(jnp.float32)
    grad_values = jnp.einsum("hqk,qhe->khe", weights_b, grad_f)
    grad_mix = jnp.einsum("qhe,khe->hqk", grad_f, value_rows.astype(jnp.float32))
    centre = jnp.sum(grad_mix * weights, axis=-1, keepdims=True)
    grad_scores = (weights * (grad_mix - centre) * score_scale).astype(jnp.bfloat16).astype(jnp.float32)
    grad_queries = jnp.einsum("hqk,khe->qhe", grad_scores, key_rows.astype(jnp.float32))
    grad_keys = jnp.einsum("hqk,qhe->khe", grad_scores, queries.astype(jnp.float32))
    return grad_queries.astype(jnp.bfloat16), grad_keys.astype(jnp.bfloat16), grad_values.astype(jnp.bfloat16)


def reference(qkv, text_kv, clip_blocks, text_count, dest_group, out_weight, grad_out):
    clip_total = qkv.shape[0]
    clip_len = qkv.shape[1]
    txt_len = text_kv.shape[1]
    head_width = out_weight.shape[0]
    model_width = out_weight.shape[1]
    placed_at = (dest_group * CPG + jnp.arange(clip_total, dtype=jnp.int32) % CPG).astype(jnp.int32)
    grad_source = grad_out[placed_at]
    positions = jnp.arange(clip_len, dtype=jnp.int32)
    text_positions = jnp.arange(txt_len, dtype=jnp.int32)

    def one_clip(running, inputs):
        video_clip, text_clip, blocks, text_live, grad_here = inputs
        video_clip = video_clip.reshape(clip_len, 3, HEADS, HEAD)
        text_clip = text_clip.reshape(txt_len, 2, HEADS, HEAD)
        live_query = positions < BLK * blocks
        live_key = jnp.concatenate([live_query, text_positions < text_live])
        queries = video_clip[:, 0]
        key_rows = jnp.concatenate([video_clip[:, 1], text_clip[:, 0]], axis=0)
        value_rows = jnp.concatenate([video_clip[:, 2], text_clip[:, 1]], axis=0)
        attended, weights = attend(queries, key_rows, value_rows, live_query, live_key)
        att_rows = attended.reshape(clip_len, head_width)
        output_rows = jnp.dot(att_rows, out_weight, preferred_element_type=jnp.float32).astype(jnp.bfloat16)
        grad_att = jnp.dot(grad_here, out_weight.T, preferred_element_type=jnp.float32)
        grad_att = grad_att * live_query[:, None].astype(jnp.float32)
        grad_att = grad_att.astype(jnp.bfloat16).reshape(clip_len, HEADS, HEAD)
        running = running + jnp.dot(att_rows.T, grad_here, preferred_element_type=jnp.float32)
        grad_queries, grad_keys, grad_values = attend_back(queries, key_rows, value_rows, weights, grad_att)
        grad_video = jnp.stack([grad_queries, grad_keys[:clip_len], grad_values[:clip_len]], axis=1)
        grad_video = grad_video.reshape(clip_len, 3 * head_width)
        grad_txt = jnp.stack([grad_keys[clip_len:], grad_values[clip_len:]], axis=1).reshape(txt_len, 2 * head_width)
        return running, (output_rows, grad_video, grad_txt)

    start_sum = jnp.zeros((head_width, model_width), jnp.float32)
    running, results = lax.scan(one_clip, start_sum, (qkv, text_kv, clip_blocks, text_count, grad_source))
    output_rows, grad_video, grad_txt = results
    out = jnp.zeros_like(output_rows).at[placed_at].set(output_rows)
    grad_qkv = jnp.zeros_like(grad_video).at[placed_at].set(grad_video)
    grad_text = jnp.zeros_like(grad_txt).at[placed_at].set(grad_txt)
    return out, grad_qkv, grad_text, running / clip_total
```

```python
import functools

import jax
import jax.numpy as jnp
from jax import lax
from jax.experimental import pallas as pl
from jax.experimental.pallas import tpu as pltpu
from jax.sharding import PartitionSpec as P

HEAD = 128
HEADS = 16
BLK = 256
GROUPS = 8
PLACES = 4
TOK = 64
TXT_DEV = 16
VIDEO = TOK * HEADS
TEXT = TXT_DEV * HEADS
KEYS = VIDEO + TEXT
HW = HEADS * HEAD
D = 3072
ROWS = 3 * TOK + 2 * TXT_DEV
SCALE = HEAD ** (-0.5)
LOG2E = 1.4426950408889634
NEG_FILL = -1e30
MESH = pl.DeviceIdType.MESH
BF = jnp.bfloat16
F32 = jnp.float32


def dot_nt(a, b):
    return lax.dot_general(a, b, (((1,), (1,)), ((), ())), preferred_element_type=F32)


def dot_nn(a, b):
    return lax.dot_general(a, b, (((1,), (0,)), ((), ())), preferred_element_type=F32)


def wait_for(ref, sem):
    pltpu.make_async_copy(ref, ref, sem).wait()


def source_group(dest_ref, group, place):
    found = jnp.int32(0)
    for g in range(GROUPS):
        found = jnp.where(dest_ref[g * PLACES + place] == group, g, found)
    return found


def relay_group(seat):
    return lax.rem(seat, 2) * 4 + lax.rem(seat // 2, 4)


def enter(others):
    barrier = pltpu.get_barrier_semaphore()
    g, s = lax.axis_index("grp"), lax.axis_index("seq")
    me = g * HEADS + s

    def greet(step, carry):
        other = lax.rem(me + step, GROUPS * HEADS)
        pl.semaphore_signal(
            barrier, inc=1, device_id=(other // HEADS, lax.rem(other, HEADS)), device_id_type=MESH
        )
        return carry

    lax.fori_loop(1, GROUPS * HEADS, greet, 0)
    pl.semaphore_wait(barrier, GROUPS * HEADS - 1)


def move_kernel(
    dest_ref, blocks_ref, qkv_ref, text_ref, grad_ref, weight_hbm,
    q_out, k_out, v_out, g_out,
    pack, relay0, relay1, relay2, relay3, sorted_, landed, weight, gpack, glanded,
    send1, recv1, send2, recv2, send3, recv3, wsem,
):
    g, s = lax.axis_index("grp"), lax.axis_index("seq")
    relays = (relay0, relay1, relay2, relay3)
    load = pltpu.make_async_copy(weight_hbm, weight, wsem)
    load.start()
    enter(None)
    relay = relay_group(s)
    half = s // 8
    home = relay == g

    for j in range(PLACES):
        def fill(h, carry):
            for t in range(3):
                pack[j, h, t * TOK:(t + 1) * TOK, :] = qkv_ref[
                    j, :, pl.ds(pl.multiple_of(t * HW + h * HEAD, HEAD), HEAD)
                ]
            for t in range(2):
                at = 3 * TOK + t * TXT_DEV
                pack[j, h, at:at + TXT_DEV, :] = text_ref[
                    j, :, pl.ds(pl.multiple_of(t * HW + h * HEAD, HEAD), HEAD)
                ]
            return carry

        lax.fori_loop(0, HEADS, fill, 0)

        def push(h):
            return pltpu.make_async_remote_copy(
                src_ref=pack.at[j, h], dst_ref=relays[j].at[g, half],
                send_sem=send1.at[j], recv_sem=recv1.at[j],
                device_id=(relay, h), device_id_type=MESH,
            )

        def spread(step, carry):
            push(lax.bitwise_xor(s, step)).start()
            return carry

        lax.fori_loop(1, HEADS, spread, 0)

        @pl.when(home)
        def _():
            pltpu.make_async_copy(pack.at[j, s], relays[j].at[g, half], recv1.at[j]).start()

        @pl.when(jnp.logical_not(home))
        def _():
            push(s).start()

    load.wait()
    grads = grad_ref[...].reshape(PLACES * TOK, D)
    live = []
    for j in range(PLACES):
        blocks = blocks_ref[source_group(dest_ref, g, j) * PLACES + j]
        live.append(jnp.where(s // 4 < blocks, 1.0, 0.0).astype(F32))

    def project(pair, carry):
        rows = pl.ds(pl.multiple_of(pair * 2 * HEAD, 2 * HEAD), 2 * HEAD)
        value = dot_nt(grads, weight[rows, :])
        for j in range(PLACES):
            part = (value[j * TOK:(j + 1) * TOK] * live[j]).astype(BF)
            gpack[2 * pair, j] = part[:, :HEAD]
            gpack[2 * pair + 1, j] = part[:, HEAD:]
        return carry

    lax.fori_loop(0, HEADS // 2, project, 0)

    def spread_g(step, carry):
        h = lax.bitwise_xor(s, step)
        pltpu.make_async_remote_copy(
            src_ref=gpack.at[h], dst_ref=glanded.at[s], send_sem=send3, recv_sem=recv3,
            device_id=(g, h), device_id_type=MESH,
        ).start()
        return carry

    lax.fori_loop(1, HEADS, spread_g, 0)
    glanded[s] = gpack[s]

    for j in range(PLACES):
        wait_for(relays[j], recv1.at[j])

        def regroup(step, carry):
            d = lax.bitwise_xor(g, step)
            came = source_group(dest_ref, d, j)
            sorted_[j, step] = relays[j][came]
            pltpu.make_async_remote_copy(
                src_ref=sorted_.at[j, step], dst_ref=landed.at[j, g],
                send_sem=send2.at[j], recv_sem=recv2.at[j],
                device_id=(d, s), device_id_type=MESH,
            ).start()
            return carry

        lax.fori_loop(1, GROUPS, regroup, 0)
        landed[j, g] = relays[j][source_group(dest_ref, g, j)]

    wait_for(glanded.at[pl.ds(1, HEADS - 1)], recv3)
    for r in range(HEADS):
        for j in range(PLACES):
            g_out[j, r * TOK:(r + 1) * TOK, :] = glanded[r, j]

    for j in range(PLACES):
        wait_for(landed.at[j, pl.ds(1, GROUPS - 1)], recv2.at[j])
        for r in range(HEADS):
            m, z = (r % 2) * 4 + (r // 2) % 4, r // 8
            q_out[j, r * TOK:(r + 1) * TOK, :] = landed[j, m, z, 0:TOK, :]
            k_out[j, r * TOK:(r + 1) * TOK, :] = landed[j, m, z, TOK:2 * TOK, :]
            v_out[j, r * TOK:(r + 1) * TOK, :] = landed[j, m, z, 2 * TOK:3 * TOK, :]
            lo = VIDEO + r * TXT_DEV
            k_out[j, lo:lo + TXT_DEV, :] = landed[j, m, z, 3 * TOK:3 * TOK + TXT_DEV, :]
            v_out[j, lo:lo + TXT_DEV, :] = landed[j, m, z, 3 * TOK + TXT_DEV:ROWS, :]

    for j in range(PLACES):
        @pl.when(home)
        def _():
            wait_for(pack.at[j, pl.ds(1, HEADS - 1)], send1.at[j])

        @pl.when(jnp.logical_not(home))
        def _():
            wait_for(pack.at[j], send1.at[j])

        wait_for(sorted_.at[j, pl.ds(1, GROUPS - 1)], send2.at[j])
    wait_for(gpack.at[pl.ds(1, HEADS - 1)], send3)


def move(dest_group, clip_blocks, qkv, text_kv, grad_out, out_weight):
    smem = pl.BlockSpec(memory_space=pltpu.SMEM)
    vmem = pl.BlockSpec(memory_space=pltpu.VMEM)
    relay = pltpu.VMEM((GROUPS, 2, ROWS, HEAD), BF)
    return pl.pallas_call(
        move_kernel,
        out_shape=(
            jax.ShapeDtypeStruct((PLACES, VIDEO, HEAD), BF),
            jax.ShapeDtypeStruct((PLACES, KEYS, HEAD), BF),
            jax.ShapeDtypeStruct((PLACES, KEYS, HEAD), BF),
            jax.ShapeDtypeStruct((PLACES, VIDEO, HEAD), BF),
        ),
        in_specs=[smem, smem, vmem, vmem, vmem, pl.BlockSpec(memory_space=pl.ANY)],
        out_specs=(vmem, vmem, vmem, vmem),
        scratch_shapes=[
            pltpu.VMEM((PLACES, HEADS, ROWS, HEAD), BF),
            relay, relay, relay, relay,
            pltpu.VMEM((PLACES, GROUPS, 2, ROWS, HEAD), BF),
            pltpu.VMEM((PLACES, GROUPS, 2, ROWS, HEAD), BF),
            pltpu.VMEM((HW, D), BF),
            pltpu.VMEM((HEADS, PLACES, TOK, HEAD), BF),
            pltpu.VMEM((HEADS, PLACES, TOK, HEAD), BF),
            pltpu.SemaphoreType.DMA((PLACES,)),
            pltpu.SemaphoreType.DMA((PLACES,)),
            pltpu.SemaphoreType.DMA((PLACES,)),
            pltpu.SemaphoreType.DMA((PLACES,)),
            pltpu.SemaphoreType.DMA,
            pltpu.SemaphoreType.DMA,
            pltpu.SemaphoreType.DMA,
        ],
        compiler_params=pltpu.CompilerParams(
            collective_id=0, has_side_effects=True, vmem_limit_bytes=56 * 1024 * 1024
        ),
        name="move",
    )(dest_group, clip_blocks, qkv, text_kv, grad_out, out_weight)


def attend_kernel(
    here_ref, q_ref, k_ref, v_ref, g_ref, o_ref, dq_ref, dk_ref, dv_ref, kt, vt, bias, dk_acc, dv_acc
):
    j = pl.program_id(0)
    blocks = here_ref[0, j]
    count = here_ref[1, j]
    kt[...] = k_ref[0].T
    vt[...] = v_ref[0].T
    row = lax.broadcasted_iota(jnp.int32, (KEYS, 2 * HEAD), 0)
    dead = jnp.logical_or(
        jnp.logical_and(row >= blocks * BLK, row < VIDEO), row >= VIDEO + count
    )
    bias[...] = jnp.where(dead, NEG_FILL, 0.0)
    dk_acc[...] = jnp.zeros_like(dk_acc)
    dv_acc[...] = jnp.zeros_like(dv_acc)

    def block(i, carry):
        at = pl.ds(pl.multiple_of(i * BLK, BLK), BLK)
        q = q_ref[0, at, :]
        g = g_ref[0, at, :]
        st = dot_nt(k_ref[0], q) + bias[...]
        top = jnp.max(st, axis=0, keepdims=True)
        e = jnp.exp2((st - top) * (SCALE * LOG2E))
        w = e * (1.0 / jnp.sum(e, axis=0, keepdims=True))
        wb = w.astype(BF)
        o_ref[0, at, :] = dot_nn(vt[...], wb).T.astype(BF)
        dv_acc[...] += dot_nn(wb, g)
        dp = dot_nt(v_ref[0], g)
        centre = jnp.sum(dp * w, axis=0, keepdims=True)
        ds = (w * (dp - centre) * SCALE).astype(BF)
        dq_ref[0, at, :] = dot_nn(kt[...], ds).T.astype(BF)
        dk_acc[...] += dot_nn(ds, q)
        return carry

    def blank(i, carry):
        at = pl.ds(pl.multiple_of(i * BLK, BLK), BLK)
        o_ref[0, at, :] = jnp.zeros((BLK, HEAD), BF)
        dq_ref[0, at, :] = jnp.zeros((BLK, HEAD), BF)
        return carry

    lax.fori_loop(0, blocks, block, 0)
    lax.fori_loop(blocks, VIDEO // BLK, blank, 0)
    dk_ref[0] = dk_acc[...].astype(BF)
    dv_ref[0] = dv_acc[...].astype(BF)


def attend(here, q, k, v, g):
    def spec(rows):
        return pl.BlockSpec((1, rows, HEAD), lambda j, here: (j, 0, 0))

    return pl.pallas_call(
        attend_kernel,
        out_shape=(
            jax.ShapeDtypeStruct((PLACES, VIDEO, HEAD), BF),
            jax.ShapeDtypeStruct((PLACES, VIDEO, HEAD), BF),
            jax.ShapeDtypeStruct((PLACES, KEYS, HEAD), BF),
            jax.ShapeDtypeStruct((PLACES, KEYS, HEAD), BF),
        ),
        grid_spec=pltpu.PrefetchScalarGridSpec(
            num_scalar_prefetch=1,
            grid=(PLACES,),
            in_specs=[spec(VIDEO), spec(KEYS), spec(KEYS), spec(VIDEO)],
            out_specs=(spec(VIDEO), spec(VIDEO), spec(KEYS), spec(KEYS)),
            scratch_shapes=[
                pltpu.VMEM((HEAD, KEYS), BF),
                pltpu.VMEM((HEAD, KEYS), BF),
                pltpu.VMEM((KEYS, 2 * HEAD), F32),
                pltpu.VMEM((KEYS, HEAD), F32),
                pltpu.VMEM((KEYS, HEAD), F32),
            ],
        ),
        compiler_params=pltpu.CompilerParams(vmem_limit_bytes=48 * 1024 * 1024),
        name="attend",
    )(here, q, k, v, g)


def on_device(qkv, text_kv, clip_blocks, text_count, dest_group, out_weight, grad_out):
    own_group = lax.axis_index("grp")
    arrive = dest_group.reshape(GROUPS, PLACES).T == own_group
    blocks_here = jnp.sum(jnp.where(arrive, clip_blocks.reshape(GROUPS, PLACES).T, 0), axis=1)
    count_here = jnp.sum(jnp.where(arrive, text_count.reshape(GROUPS, PLACES).T, 0), axis=1)
    here = jnp.stack([blocks_here, count_here])
    q, k, v, g = move(dest_group, clip_blocks, qkv, text_kv, grad_out, out_weight)
    attended, dq, dk, dv = attend(here, q, k, v, g)
    attended_tok = lax.all_to_all(
        attended[:, :, None, :], "seq", split_axis=1, concat_axis=2, tiled=True
    )
    attended_rows = attended_tok.reshape(PLACES * TOK, HW)
    out = jnp.dot(attended_rows, out_weight, preferred_element_type=F32).astype(BF)
    grad_rows = grad_out.reshape(PLACES * TOK, D)
    partial_term = lax.psum_scatter(
        jnp.einsum("tr,td->rd", attended_rows, grad_rows, preferred_element_type=F32).astype(BF),
        "seq", scatter_dimension=0, tiled=True,
    )
    grad_weight = lax.psum_scatter(partial_term, "grp", scatter_dimension=1, tiled=True).astype(
        F32
    ) / (PLACES * GROUPS)
    grad_video = jnp.stack([dq, dk[:, :VIDEO], dv[:, :VIDEO]], axis=2)[:, :, :, None, :]
    grad_txt = jnp.stack([dk[:, VIDEO:], dv[:, VIDEO:]], axis=2)[:, :, :, None, :]
    back_video = lax.all_to_all(grad_video, "seq", split_axis=1, concat_axis=3, tiled=True)
    back_text = lax.all_to_all(grad_txt, "seq", split_axis=1, concat_axis=3, tiled=True)
    return (
        out.reshape(PLACES, TOK, D),
        back_video.reshape(PLACES, TOK, 3 * HW),
        back_text.reshape(PLACES, TXT_DEV, 2 * HW),
        grad_weight,
    )


def solution(mesh):
    return jax.shard_map(
        on_device,
        mesh=mesh,
        in_specs=(
            P("grp", "seq", None),
            P("grp", "seq", None),
            P(),
            P(),
            P(),
            P(),
            P("grp", "seq", None),
        ),
        out_specs=(
            P("grp", "seq", None),
            P("grp", "seq", None),
            P("grp", "seq", None),
            P("seq", "grp"),
        ),
        check_vma=False,
    )
```

```python
import functools

import jax
import jax.numpy as jnp
from jax import lax
from jax.experimental import pallas as pl
from jax.experimental.pallas import tpu as pltpu
from jax.sharding import PartitionSpec as P

HEAD = 128
HEADS = 16
BLK = 256
GROUPS = 8
PLACES = 4
TOK = 64
TXT_DEV = 16
VIDEO = TOK * HEADS
TEXT = TXT_DEV * HEADS
KEYS = VIDEO + TEXT
HW = HEADS * HEAD
D = 3072
ROWS = 3 * TOK + 2 * TXT_DEV
SCALE = HEAD ** (-0.5)
LOG2E = 1.4426950408889634
NEG_FILL = -1e30
MESH = pl.DeviceIdType.MESH
BF = jnp.bfloat16
F32 = jnp.float32


def dot_nt(a, b):
    return lax.dot_general(a, b, (((1,), (1,)), ((), ())), preferred_element_type=F32)


def dot_nn(a, b):
    return lax.dot_general(a, b, (((1,), (0,)), ((), ())), preferred_element_type=F32)


def wait_for(ref, sem):
    pltpu.make_async_copy(ref, ref, sem).wait()


def source_group(dest_ref, group, place):
    found = jnp.int32(0)
    for g in range(GROUPS):
        found = jnp.where(dest_ref[g * PLACES + place] == group, g, found)
    return found


def relay_group(seat):
    return lax.rem(seat, 2) * 4 + lax.rem(seat // 2, 4)


def enter(others):
    barrier = pltpu.get_barrier_semaphore()
    g, s = lax.axis_index("grp"), lax.axis_index("seq")
    me = g * HEADS + s

    def greet(step, carry):
        other = lax.rem(me + step, GROUPS * HEADS)
        pl.semaphore_signal(
            barrier, inc=1, device_id=(other // HEADS, lax.rem(other, HEADS)), device_id_type=MESH
        )
        return carry

    lax.fori_loop(1, GROUPS * HEADS, greet, 0)
    pl.semaphore_wait(barrier, GROUPS * HEADS - 1)


def move_kernel(
    dest_ref, blocks_ref, qkv_ref, text_ref, grad_ref, weight_hbm,
    q_out, k_out, v_out, g_out,
    pack, relay0, relay1, relay2, relay3, sorted_, landed, weight, gpack, glanded,
    send1, recv1, send2, recv2, send3, recv3, wsem,
):
    g, s = lax.axis_index("grp"), lax.axis_index("seq")
    relays = (relay0, relay1, relay2, relay3)
    load = pltpu.make_async_copy(weight_hbm, weight, wsem)
    load.start()
    enter(None)
    relay = relay_group(s)
    half = s // 8
    home = relay == g

    for j in range(PLACES):
        def fill(h, carry):
            for t in range(3):
                pack[j, h, t * TOK:(t + 1) * TOK, :] = qkv_ref[
                    j, :, pl.ds(pl.multiple_of(t * HW + h * HEAD, HEAD), HEAD)
                ]
            for t in range(2):
                at = 3 * TOK + t * TXT_DEV
                pack[j, h, at:at + TXT_DEV, :] = text_ref[
                    j, :, pl.ds(pl.multiple_of(t * HW + h * HEAD, HEAD), HEAD)
                ]
            return carry

        lax.fori_loop(0, HEADS, fill, 0)

        def push(h):
            return pltpu.make_async_remote_copy(
                src_ref=pack.at[j, h], dst_ref=relays[j].at[g, half],
                send_sem=send1.at[j], recv_sem=recv1.at[j],
                device_id=(relay, h), device_id_type=MESH,
            )

        def spread(step, carry):
            push(lax.bitwise_xor(s, step)).start()
            return carry

        lax.fori_loop(1, HEADS, spread, 0)

        @pl.when(home)
        def _():
            pltpu.make_async_copy(pack.at[j, s], relays[j].at[g, half], recv1.at[j]).start()

        @pl.when(jnp.logical_not(home))
        def _():
            push(s).start()

    load.wait()
    grads = grad_ref[...].reshape(PLACES * TOK, D)
    live = []
    for j in range(PLACES):
        blocks = blocks_ref[source_group(dest_ref, g, j) * PLACES + j]
        live.append(jnp.where(s // 4 < blocks, 1.0, 0.0).astype(F32))

    def project(pair, carry):
        rows = pl.ds(pl.multiple_of(pair * 2 * HEAD, 2 * HEAD), 2 * HEAD)
        value = dot_nt(grads, weight[rows, :])
        for j in range(PLACES):
            part = (value[j * TOK:(j + 1) * TOK] * live[j]).astype(BF)
            gpack[2 * pair, j] = part[:, :HEAD]
            gpack[2 * pair + 1, j] = part[:, HEAD:]
        return carry

    lax.fori_loop(0, HEADS // 2, project, 0)

    def spread_g(step, carry):
        h = lax.bitwise_xor(s, step)
        pltpu.make_async_remote_copy(
            src_ref=gpack.at[h], dst_ref=glanded.at[s], send_sem=send3, recv_sem=recv3,
            device_id=(g, h), device_id_type=MESH,
        ).start()
        return carry

    lax.fori_loop(1, HEADS, spread_g, 0)
    glanded[s] = gpack[s]

    for j in range(PLACES):
        wait_for(relays[j], recv1.at[j])

        def regroup(step, carry):
            d = lax.bitwise_xor(g, step)
            came = source_group(dest_ref, d, j)
            sorted_[j, step] = relays[j][came]
            pltpu.make_async_remote_copy(
                src_ref=sorted_.at[j, step], dst_ref=landed.at[j, g],
                send_sem=send2.at[j], recv_sem=recv2.at[j],
                device_id=(d, s), device_id_type=MESH,
            ).start()
            return carry

        lax.fori_loop(1, GROUPS, regroup, 0)
        landed[j, g] = relays[j][source_group(dest_ref, g, j)]

    wait_for(glanded.at[pl.ds(1, HEADS - 1)], recv3)
    for r in range(HEADS):
        for j in range(PLACES):
            g_out[j, r * TOK:(r + 1) * TOK, :] = glanded[r, j]

    for j in range(PLACES):
        wait_for(landed.at[j, pl.ds(1, GROUPS - 1)], recv2.at[j])
        for r in range(HEADS):
            m, z = (r % 2) * 4 + (r // 2) % 4, r // 8
            q_out[j, r * TOK:(r + 1) * TOK, :] = landed[j, m, z, 0:TOK, :]
            k_out[j, r * TOK:(r + 1) * TOK, :] = landed[j, m, z, TOK:2 * TOK, :]
            v_out[j, r * TOK:(r + 1) * TOK, :] = landed[j, m, z, 2 * TOK:3 * TOK, :]
            lo = VIDEO + r * TXT_DEV
            k_out[j, lo:lo + TXT_DEV, :] = landed[j, m, z, 3 * TOK:3 * TOK + TXT_DEV, :]
            v_out[j, lo:lo + TXT_DEV, :] = landed[j, m, z, 3 * TOK + TXT_DEV:ROWS, :]

    for j in range(PLACES):
        @pl.when(home)
        def _():
            wait_for(pack.at[j, pl.ds(1, HEADS - 1)], send1.at[j])

        @pl.when(jnp.logical_not(home))
        def _():
            wait_for(pack.at[j], send1.at[j])

        wait_for(sorted_.at[j, pl.ds(1, GROUPS - 1)], send2.at[j])
    wait_for(gpack.at[pl.ds(1, HEADS - 1)], send3)


def move(dest_group, clip_blocks, qkv, text_kv, grad_out, out_weight):
    smem = pl.BlockSpec(memory_space=pltpu.SMEM)
    vmem = pl.BlockSpec(memory_space=pltpu.VMEM)
    relay = pltpu.VMEM((GROUPS, 2, ROWS, HEAD), BF)
    return pl.pallas_call(
        move_kernel,
        out_shape=(
            jax.ShapeDtypeStruct((PLACES, VIDEO, HEAD), BF),
            jax.ShapeDtypeStruct((PLACES, KEYS, HEAD), BF),
            jax.ShapeDtypeStruct((PLACES, KEYS, HEAD), BF),
            jax.ShapeDtypeStruct((PLACES, VIDEO, HEAD), BF),
        ),
        in_specs=[smem, smem, vmem, vmem, vmem, pl.BlockSpec(memory_space=pl.ANY)],
        out_specs=(vmem, vmem, vmem, vmem),
        scratch_shapes=[
            pltpu.VMEM((PLACES, HEADS, ROWS, HEAD), BF),
            relay, relay, relay, relay,
            pltpu.VMEM((PLACES, GROUPS, 2, ROWS, HEAD), BF),
            pltpu.VMEM((PLACES, GROUPS, 2, ROWS, HEAD), BF),
            pltpu.VMEM((HW, D), BF),
            pltpu.VMEM((HEADS, PLACES, TOK, HEAD), BF),
            pltpu.VMEM((HEADS, PLACES, TOK, HEAD), BF),
            pltpu.SemaphoreType.DMA((PLACES,)),
            pltpu.SemaphoreType.DMA((PLACES,)),
            pltpu.SemaphoreType.DMA((PLACES,)),
            pltpu.SemaphoreType.DMA((PLACES,)),
            pltpu.SemaphoreType.DMA,
            pltpu.SemaphoreType.DMA,
            pltpu.SemaphoreType.DMA,
        ],
        compiler_params=pltpu.CompilerParams(
            collective_id=0, has_side_effects=True, vmem_limit_bytes=56 * 1024 * 1024
        ),
        name="move",
    )(dest_group, clip_blocks, qkv, text_kv, grad_out, out_weight)


def attend_kernel(
    here_ref, q_ref, k_ref, v_ref, g_ref, o_ref, dq_ref, dk_ref, dv_ref, kt, vt, bias, dk_acc, dv_acc
):
    j = pl.program_id(0)
    blocks = here_ref[0, j]
    count = here_ref[1, j]
    kt[...] = k_ref[0].T
    vt[...] = v_ref[0].T
    row = lax.broadcasted_iota(jnp.int32, (KEYS, 2 * HEAD), 0)
    dead = jnp.logical_or(
        jnp.logical_and(row >= blocks * BLK, row < VIDEO), row >= VIDEO + count
    )
    bias[...] = jnp.where(dead, NEG_FILL, 0.0)
    dk_acc[...] = jnp.zeros_like(dk_acc)
    dv_acc[...] = jnp.zeros_like(dv_acc)

    def block(i, carry):
        at = pl.ds(pl.multiple_of(i * BLK, BLK), BLK)
        q = q_ref[0, at, :]
        g = g_ref[0, at, :]
        st = dot_nt(k_ref[0], q) + bias[...]
        top = jnp.max(st, axis=0, keepdims=True)
        e = jnp.exp2((st - top) * (SCALE * LOG2E))
        w = e * (1.0 / jnp.sum(e, axis=0, keepdims=True))
        wb = w.astype(BF)
        o_ref[0, at, :] = dot_nn(vt[...], wb).T.astype(BF)
        dv_acc[...] += dot_nn(wb, g)
        dp = dot_nt(v_ref[0], g)
        centre = jnp.sum(dp * w, axis=0, keepdims=True)
        ds = (w * (dp - centre) * SCALE).astype(BF)
        dq_ref[0, at, :] = dot_nn(kt[...], ds).T.astype(BF)
        dk_acc[...] += dot_nn(ds, q)
        return carry

    def blank(i, carry):
        at = pl.ds(pl.multiple_of(i * BLK, BLK), BLK)
        o_ref[0, at, :] = jnp.zeros((BLK, HEAD), BF)
        dq_ref[0, at, :] = jnp.zeros((BLK, HEAD), BF)
        return carry

    lax.fori_loop(0, blocks, block, 0)
    lax.fori_loop(blocks, VIDEO // BLK, blank, 0)
    dk_ref[0] = dk_acc[...].astype(BF)
    dv_ref[0] = dv_acc[...].astype(BF)


def attend(here, q, k, v, g):
    def spec(rows):
        return pl.BlockSpec((1, rows, HEAD), lambda j, here: (j, 0, 0))

    return pl.pallas_call(
        attend_kernel,
        out_shape=(
            jax.ShapeDtypeStruct((PLACES, VIDEO, HEAD), BF),
            jax.ShapeDtypeStruct((PLACES, VIDEO, HEAD), BF),
            jax.ShapeDtypeStruct((PLACES, KEYS, HEAD), BF),
            jax.ShapeDtypeStruct((PLACES, KEYS, HEAD), BF),
        ),
        grid_spec=pltpu.PrefetchScalarGridSpec(
            num_scalar_prefetch=1,
            grid=(PLACES,),
            in_specs=[spec(VIDEO), spec(KEYS), spec(KEYS), spec(VIDEO)],
            out_specs=(spec(VIDEO), spec(VIDEO), spec(KEYS), spec(KEYS)),
            scratch_shapes=[
                pltpu.VMEM((HEAD, KEYS), BF),
                pltpu.VMEM((HEAD, KEYS), BF),
                pltpu.VMEM((KEYS, 2 * HEAD), F32),
                pltpu.VMEM((KEYS, HEAD), F32),
                pltpu.VMEM((KEYS, HEAD), F32),
            ],
        ),
        compiler_params=pltpu.CompilerParams(vmem_limit_bytes=48 * 1024 * 1024),
        name="attend",
    )(here, q, k, v, g)


def dot_tn(a, b):
    return lax.dot_general(a, b, (((0,), (0,)), ((), ())), preferred_element_type=F32)


X1, X2, Y1, Y2, Z1, Z2 = range(6)
ORDERS = (
    (X1, Y1, Z1, X2, Y2, Z2),
    (Y1, Z1, X2, Y2, Z2, X1),
    (Z1, X2, Y2, Z2, X1, Y1),
    (X2, Y2, Z2, X1, Y1, Z1),
    (Y2, Z2, X1, Y1, Z1, X2),
    (Z2, X1, Y1, Z1, X2, Y2),
)
PARTS = 6
CHIPS = 64
EARLY = 8


def ring_bits(u):
    high = u // 2
    return lax.bitwise_xor(lax.rem(u, 2), high), high


def cube_bits(head_pair, column_block):
    x1, x2 = ring_bits(lax.rem(head_pair, 4))
    y1, y2 = ring_bits(lax.rem(column_block, 4))
    z1, z2 = ring_bits(2 * (head_pair // 4) + column_block // 4)
    return x1, x2, y1, y2, z1, z2


def cube_index(bits, order, count=6):
    at = jnp.int32(0)
    for k in range(count):
        at = at + bits[order[k]] * (CHIPS // 2 >> k)
    return at


def cube_neighbour(dim, g, s):
    z_lo, y = g // 4, lax.rem(g, 4)
    z_hi, x, core = s // 8, lax.rem(s // 2, 4), lax.rem(s, 2)
    if dim == X1:
        x = lax.bitwise_xor(x, 1)
    if dim == X2:
        x = 3 - x
    if dim == Y1:
        y = lax.bitwise_xor(y, 1)
    if dim == Y2:
        y = 3 - y
    if dim in (Z1, Z2):
        z_lo = 1 - z_lo
    if dim == Z2:
        z_hi = 1 - z_hi
    return z_lo * 4 + y, (z_hi * 4 + x) * 2 + core


def finish_kernel(
    att_ref, dq_ref, dk_ref, dv_ref, grad_ref, weight_hbm,
    out_ref, gq_ref, gt_ref, gw_ref,
    alanded, afwd, gpart, pack, blanded, weight, acc, arrived, rows,
    asend, arecv, fsend, frecv, gsend, grecv, bsend, brecv, rsend, rrecv, wsem,
):
    g, s = lax.axis_index("grp"), lax.axis_index("seq")
    core = lax.rem(s, 2)
    partner = lax.bitwise_xor(s, 1)
    load = pltpu.make_async_copy(weight_hbm, weight, wsem)
    load.start()

    barrier = pltpu.get_barrier_semaphore()

    def greet(step, carry):
        pl.semaphore_signal(
            barrier, inc=1, device_id=(g, lax.bitwise_xor(s, step)), device_id_type=MESH
        )
        return carry

    lax.fori_loop(1, HEADS, greet, 0)
    for dim in (Y1, Y2, Z1, Z2):
        pl.semaphore_signal(
            barrier, inc=1, device_id=cube_neighbour(dim, g, s), device_id_type=MESH
        )
    pl.semaphore_wait(barrier, HEADS - 1 + 4)

    def token_rows(r):
        return pl.ds(pl.multiple_of(r * TOK, TOK), TOK)

    def text_rows(r):
        return pl.ds(pl.multiple_of(VIDEO + r * TXT_DEV, TXT_DEV), TXT_DEV)

    def send_att(step, carry):
        r = lax.bitwise_xor(s, step)
        pltpu.make_async_remote_copy(
            src_ref=att_ref.at[:, token_rows(r), :], dst_ref=alanded.at[s],
            send_sem=asend, recv_sem=arecv, device_id=(g, r), device_id_type=MESH,
        ).start()
        return carry

    lax.fori_loop(1, HEADS, send_att, 0)
    alanded[s] = att_ref[:, token_rows(s), :]
    lend = pltpu.make_async_remote_copy(
        src_ref=grad_ref, dst_ref=gpart, send_sem=gsend, recv_sem=grecv,
        device_id=(g, partner), device_id_type=MESH,
    )
    lend.start()

    def back(step):
        r = lax.bitwise_xor(s, step)
        return pltpu.make_async_remote_copy(
            src_ref=pack.at[r], dst_ref=blanded.at[s],
            send_sem=bsend, recv_sem=brecv.at[step], device_id=(g, r), device_id_type=MESH,
        )

    def send_back(step, carry):
        r = lax.bitwise_xor(s, step)
        for j in range(PLACES):
            pack[r, j, 0:TOK, :] = dq_ref[j, token_rows(r), :]
            pack[r, j, TOK:2 * TOK, :] = dk_ref[j, token_rows(r), :]
            pack[r, j, 2 * TOK:3 * TOK, :] = dv_ref[j, token_rows(r), :]
            pack[r, j, 3 * TOK:3 * TOK + TXT_DEV, :] = dk_ref[j, text_rows(r), :]
            pack[r, j, 3 * TOK + TXT_DEV:ROWS, :] = dv_ref[j, text_rows(r), :]
        back(step).start()
        return carry

    lax.fori_loop(1, EARLY, send_back, 0)

    wait_for(alanded.at[pl.ds(1, HEADS - 1)], arecv)

    def forward(i, carry):
        pltpu.make_async_remote_copy(
            src_ref=alanded.at[2 * i + 1 - core], dst_ref=afwd.at[i],
            send_sem=fsend, recv_sem=frecv, device_id=(g, partner), device_id_type=MESH,
        ).start()
        return carry

    lax.fori_loop(0, HEADS // 2, forward, 0)
    for h in range(HEADS):
        rows[:, h * HEAD:(h + 1) * HEAD] = alanded[h].reshape(PLACES * TOK, HEAD)
    lend.wait_recv()
    wait_for(afwd, frecv)

    def term(pair, carry):
        mine = jnp.concatenate(
            [alanded[4 * pair + 2 * i + core].reshape(PLACES * TOK, HEAD) for i in range(2)], axis=1
        )
        theirs = jnp.concatenate(
            [afwd[2 * pair + i].reshape(PLACES * TOK, HEAD) for i in range(2)], axis=1
        )
        both = jnp.concatenate([mine, theirs], axis=0)
        for c in range(4):
            columns = slice(c * 768, (c + 1) * 768)
            right = jnp.concatenate(
                [grad_ref[:, :, columns].reshape(PLACES * TOK, 768),
                 gpart[:, :, columns].reshape(PLACES * TOK, 768)], axis=0)
            value = dot_tn(both, right).astype(BF)
            for i in range(2):
                for b in range(2):
                    bits = cube_bits(2 * pair + i, jnp.int32(2 * c + b))
                    for p in range(PARTS):
                        rh, ct = p // 3, p % 3
                        top, left = i * HEAD + rh * 64, b * 384 + ct * HEAD
                        acc[p, cube_index(bits, ORDERS[p])] = value[
                            top:top + 64, left:left + HEAD
                        ]
        return carry

    lax.fori_loop(0, 4, term, 0)

    own = cube_bits(s // 2, g)

    def exchange(p, k):
        dim = ORDERS[p][k]
        size = CHIPS // 2 >> k
        start = cube_index(own, ORDERS[p], k) + (1 - own[dim]) * size
        return pltpu.make_async_remote_copy(
            src_ref=acc.at[p, pl.ds(start, size)],
            dst_ref=arrived.at[p, pl.ds(CHIPS - 2 * size, size)],
            send_sem=rsend.at[p, k], recv_sem=rrecv.at[p, k],
            device_id=cube_neighbour(dim, g, s), device_id_type=MESH,
        )

    for p in range(PARTS):
        exchange(p, 0).start()
    lax.fori_loop(EARLY, HEADS, send_back, 0)

    load.wait()

    def project(c, carry):
        columns = pl.ds(pl.multiple_of(c * 512, 512), 512)
        value = dot_nn(rows[...], weight[:, columns]).astype(BF)
        out_ref[:, :, columns] = value.reshape(PLACES, TOK, 512)
        return carry

    lax.fori_loop(0, D // 512, project, 0)

    def place(h, block):
        for j in range(PLACES):
            for t in range(3):
                gq_ref[j, :, pl.ds(pl.multiple_of(t * HW + h * HEAD, HEAD), HEAD)] = block[
                    j, t * TOK:(t + 1) * TOK
                ]
            for t in range(2):
                lo = 3 * TOK + t * TXT_DEV
                gt_ref[j, :, pl.ds(pl.multiple_of(t * HW + h * HEAD, HEAD), HEAD)] = block[
                    j, lo:lo + TXT_DEV
                ]

    for j in range(PLACES):
        for t, ref in enumerate((dq_ref, dk_ref, dv_ref)):
            gq_ref[j, :, pl.ds(pl.multiple_of(t * HW + s * HEAD, HEAD), HEAD)] = ref[
                j, token_rows(s), :
            ]
        for t, ref in enumerate((dk_ref, dv_ref)):
            gt_ref[j, :, pl.ds(pl.multiple_of(t * HW + s * HEAD, HEAD), HEAD)] = ref[
                j, text_rows(s), :
            ]

    for k in range(6):
        size = CHIPS // 2 >> k
        for p in range(PARTS):
            exchange(p, k).wait_recv()
            start = cube_index(own, ORDERS[p], k + 1)

            if k < 5:
                chunk = min(size, 4)

                def add(i, carry):
                    at = pl.ds(start + i * chunk, chunk)
                    come = pl.ds(CHIPS - 2 * size + i * chunk, chunk)
                    acc[p, at] = (acc[p, at].astype(F32) + arrived[p, come].astype(F32)).astype(BF)
                    return carry

                lax.fori_loop(0, size // chunk, add, 0)
                exchange(p, k + 1).start()
            else:
                rh, ct = p // 3, p % 3
                total = acc[p, start].astype(F32) + arrived[p, CHIPS - 2].astype(F32)
                gw_ref[rh * 64:(rh + 1) * 64, ct * HEAD:(ct + 1) * HEAD] = total * (
                    1.0 / (PLACES * GROUPS)
                )

    def collect(step, carry):
        back(step).wait_recv()
        h = lax.bitwise_xor(s, step)
        place(h, blanded[h])
        return carry

    lax.fori_loop(1, HEADS, collect, 0)

    wait_for(alanded.at[pl.ds(1, HEADS - 1)], asend)
    lend.wait_send()
    wait_for(afwd, fsend)
    wait_for(pack.at[pl.ds(1, HEADS - 1)], bsend)
    for k in range(6):
        for p in range(PARTS):
            exchange(p, k).wait_send()


def finish(attended, dq, dk, dv, grad_out, out_weight):
    vmem = pl.BlockSpec(memory_space=pltpu.VMEM)
    dma = pltpu.SemaphoreType.DMA
    return pl.pallas_call(
        finish_kernel,
        out_shape=(
            jax.ShapeDtypeStruct((PLACES, TOK, D), BF),
            jax.ShapeDtypeStruct((PLACES, TOK, 3 * HW), BF),
            jax.ShapeDtypeStruct((PLACES, TXT_DEV, 2 * HW), BF),
            jax.ShapeDtypeStruct((HEAD, D // GROUPS), F32),
        ),
        in_specs=[vmem] * 5 + [pl.BlockSpec(memory_space=pl.ANY)],
        out_specs=(vmem,) * 4,
        scratch_shapes=[
            pltpu.VMEM((HEADS, PLACES, TOK, HEAD), BF),
            pltpu.VMEM((HEADS // 2, PLACES, TOK, HEAD), BF),
            pltpu.VMEM((PLACES, TOK, D), BF),
            pltpu.VMEM((HEADS, PLACES, ROWS, HEAD), BF),
            pltpu.VMEM((HEADS, PLACES, ROWS, HEAD), BF),
            pltpu.VMEM((HW, D), BF),
            pltpu.VMEM((PARTS, CHIPS, 64, HEAD), BF),
            pltpu.VMEM((PARTS, CHIPS, 64, HEAD), BF),
            pltpu.VMEM((PLACES * TOK, HW), BF),
            dma, dma, dma, dma, dma, dma, dma,
            dma((HEADS,)), dma((PARTS, 6)), dma((PARTS, 6)), dma,
        ],
        compiler_params=pltpu.CompilerParams(
            collective_id=1, has_side_effects=True, vmem_limit_bytes=60 * 1024 * 1024
        ),
        name="finish",
    )(attended, dq, dk, dv, grad_out, out_weight)


def on_device(qkv, text_kv, clip_blocks, text_count, dest_group, out_weight, grad_out):
    own_group = lax.axis_index("grp")
    arrive = dest_group.reshape(GROUPS, PLACES).T == own_group
    blocks_here = jnp.sum(jnp.where(arrive, clip_blocks.reshape(GROUPS, PLACES).T, 0), axis=1)
    count_here = jnp.sum(jnp.where(arrive, text_count.reshape(GROUPS, PLACES).T, 0), axis=1)
    here = jnp.stack([blocks_here, count_here])
    q, k, v, g = move(dest_group, clip_blocks, qkv, text_kv, grad_out, out_weight)
    attended, dq, dk, dv = attend(here, q, k, v, g)
    return finish(attended, dq, dk, dv, grad_out, out_weight)


def solution(mesh):
    return jax.shard_map(
        on_device,
        mesh=mesh,
        in_specs=(
            P("grp", "seq", None),
            P("grp", "seq", None),
            P(),
            P(),
            P(),
            P(),
            P("grp", "seq", None),
        ),
        out_specs=(
            P("grp", "seq", None),
            P("grp", "seq", None),
            P("grp", "seq", None),
            P("seq", "grp"),
        ),
        check_vma=False,
    )
```

```python
import functools

import jax
import jax.numpy as jnp
from jax import lax
from jax.experimental import pallas as pl
from jax.experimental.pallas import tpu as pltpu
from jax.sharding import PartitionSpec as P

HEAD = 128
HEADS = 16
BLK = 256
GROUPS = 8
PLACES = 4
TOK = 64
TXT_DEV = 16
VIDEO = TOK * HEADS
TEXT = TXT_DEV * HEADS
KEYS = VIDEO + TEXT
HW = HEADS * HEAD
D = 3072
ROWS = 3 * TOK + 2 * TXT_DEV
SCALE = HEAD ** (-0.5)
LOG2E = 1.4426950408889634
NEG_FILL = -1e30
MESH = pl.DeviceIdType.MESH
BF = jnp.bfloat16
F32 = jnp.float32


def dot_nt(a, b):
    return lax.dot_general(a, b, (((1,), (1,)), ((), ())), preferred_element_type=F32)


def dot_nn(a, b):
    return lax.dot_general(a, b, (((1,), (0,)), ((), ())), preferred_element_type=F32)


def wait_for(ref, sem):
    pltpu.make_async_copy(ref, ref, sem).wait()


def source_group(dest_ref, group, place):
    found = jnp.int32(0)
    for g in range(GROUPS):
        found = jnp.where(dest_ref[g * PLACES + place] == group, g, found)
    return found


def relay_group(seat):
    return lax.rem(seat, 2) * 4 + lax.rem(seat // 2, 4)


def enter():
    barrier = pltpu.get_barrier_semaphore()
    g, s = lax.axis_index("grp"), lax.axis_index("seq")
    me = g * HEADS + s

    def greet(step, carry):
        other = lax.rem(me + step, GROUPS * HEADS)
        pl.semaphore_signal(
            barrier, inc=1, device_id=(other // HEADS, lax.rem(other, HEADS)), device_id_type=MESH
        )
        return carry

    lax.fori_loop(1, GROUPS * HEADS, greet, 0)
    pl.semaphore_wait(barrier, GROUPS * HEADS - 1)


def dot_tn(a, b):
    return lax.dot_general(a, b, (((0,), (0,)), ((), ())), preferred_element_type=F32)


X1, X2, Y1, Y2, Z1, Z2 = range(6)
ORDERS = (
    (X1, Y1, Z1, X2, Y2, Z2),
    (Y1, Z1, X2, Y2, Z2, X1),
    (Z1, X2, Y2, Z2, X1, Y1),
    (X2, Y2, Z2, X1, Y1, Z1),
    (Y2, Z2, X1, Y1, Z1, X2),
    (Z2, X1, Y1, Z1, X2, Y2),
)
PARTS = 6
CHIPS = 64
COLUMNS = 512


def ring_bits(u):
    high = u // 2
    return lax.bitwise_xor(lax.rem(u, 2), high), high


def cube_bits(head_pair, column_block):
    x1, x2 = ring_bits(lax.rem(head_pair, 4))
    y1, y2 = ring_bits(lax.rem(column_block, 4))
    z1, z2 = ring_bits(2 * (head_pair // 4) + column_block // 4)
    return x1, x2, y1, y2, z1, z2


def cube_index(bits, order, count=6):
    at = jnp.int32(0)
    for k in range(count):
        at = at + bits[order[k]] * (CHIPS // 2 >> k)
    return at


def cube_neighbour(dim, g, s):
    z_lo, y = g // 4, lax.rem(g, 4)
    z_hi, x, core = s // 8, lax.rem(s // 2, 4), lax.rem(s, 2)
    if dim == X1:
        x = lax.bitwise_xor(x, 1)
    if dim == X2:
        x = 3 - x
    if dim == Y1:
        y = lax.bitwise_xor(y, 1)
    if dim == Y2:
        y = 3 - y
    if dim in (Z1, Z2):
        z_lo = 1 - z_lo
    if dim == Z2:
        z_hi = 1 - z_hi
    return z_lo * 4 + y, (z_hi * 4 + x) * 2 + core


def kernel(
    dest_ref, blocks_ref, count_ref, qkv_hbm, text_hbm, grad_hbm, weight_hbm,
    out_ref, gq_ref, gt_ref, gw_ref,
    pack, relay0, relay1, relay2, relay3, sorted_, landed, gpack, glanded,
    wide, total, q_s, k_s, v_s, g_s, kt, vt, bias, o_s, dq_s, dk_s, dv_s,
    alanded, afwd, gpart, blanded, acc, arrived, rows,
    load_sem, wide_sem, send1, recv1, send2, recv2, send3, recv3,
    asend, arecv, fsend, frecv, lend_send, lend_recv, bsend, brecv, rsend, rrecv,
):
    g, s = lax.axis_index("grp"), lax.axis_index("seq")
    core = lax.rem(s, 2)
    partner = lax.bitwise_xor(s, 1)
    relays = (relay0, relay1, relay2, relay3)
    relay = relay_group(s)
    half = s // 8
    home = relay == g
    away = jnp.logical_not(home)

    def head_columns(t, h):
        return pl.ds(pl.multiple_of(t * HW + h * HEAD, HEAD), HEAD)

    def token_rows(r):
        return pl.ds(pl.multiple_of(r * TOK, TOK), TOK)

    def text_rows(r):
        return pl.ds(pl.multiple_of(VIDEO + r * TXT_DEV, TXT_DEV), TXT_DEV)

    loads = [pltpu.make_async_copy(qkv_hbm.at[j], gq_ref.at[j], load_sem.at[j]) for j in range(PLACES)]
    loads.append(pltpu.make_async_copy(text_hbm, gt_ref, load_sem.at[PLACES]))
    loads.append(pltpu.make_async_copy(grad_hbm, out_ref, load_sem.at[PLACES + 1]))

    def widen(c):
        return pltpu.make_async_copy(
            weight_hbm.at[:, c * COLUMNS:(c + 1) * COLUMNS], wide.at[c % 2], wide_sem.at[c % 2]
        )

    for load in loads:
        load.start()
    widen(0).start()
    widen(1).start()
    enter()

    def push(j, h):
        return pltpu.make_async_remote_copy(
            src_ref=pack.at[j, h], dst_ref=relays[j].at[g, half],
            send_sem=send1.at[j], recv_sem=recv1.at[j],
            device_id=(relay, h), device_id_type=MESH,
        )

    def spread(j):
        loads[j].wait()

        def one(step, carry):
            h = lax.bitwise_xor(s, step)
            for t in range(3):
                pack[j, h, t * TOK:(t + 1) * TOK, :] = gq_ref[j, :, head_columns(t, h)]
            for t in range(2):
                at = 3 * TOK + t * TXT_DEV
                pack[j, h, at:at + TXT_DEV, :] = gt_ref[j, :, head_columns(t, h)]

            @pl.when(jnp.logical_or(step > 0, away))
            def _():
                push(j, h).start()

            return carry

        lax.fori_loop(0, HEADS, one, 0)

        @pl.when(home)
        def _():
            pltpu.make_async_copy(pack.at[j, s], relays[j].at[g, half], recv1.at[j]).start()

    def spread_done(j):
        @pl.when(home)
        def _():
            wait_for(pack.at[j, pl.ds(1, HEADS - 1)], send1.at[j])

        @pl.when(away)
        def _():
            wait_for(pack.at[j], send1.at[j])

    def regroup(j):
        wait_for(relays[j], recv1.at[j])
        if j >= 2:
            wait_for(sorted_.at[j % 2, pl.ds(1, GROUPS - 1)], send2.at[j - 2])

        def one(step, carry):
            d = lax.bitwise_xor(g, step)
            sorted_[j % 2, step] = relays[j][source_group(dest_ref, d, j)]
            pltpu.make_async_remote_copy(
                src_ref=sorted_.at[j % 2, step], dst_ref=landed.at[j, g],
                send_sem=send2.at[j], recv_sem=recv2.at[j],
                device_id=(d, s), device_id_type=MESH,
            ).start()
            return carry

        lax.fori_loop(1, GROUPS, one, 0)
        landed[j, g] = relays[j][source_group(dest_ref, g, j)]

    def project_grads():
        for c in range(D // COLUMNS):
            widen(c).wait()
            part = dot_nt(
                out_ref[:, :, c * COLUMNS:(c + 1) * COLUMNS].reshape(PLACES * TOK, COLUMNS),
                wide[c % 2],
            )
            total[...] = part if c == 0 else total[...] + part
            widen((c + 2) % (D // COLUMNS)).start()
        for j in range(PLACES):
            blocks = blocks_ref[source_group(dest_ref, g, j) * PLACES + j]
            live = jnp.where(s // 4 < blocks, 1.0, 0.0).astype(F32)
            for h in range(HEADS):
                gpack[h, j] = (
                    total[j * TOK:(j + 1) * TOK, h * HEAD:(h + 1) * HEAD] * live
                ).astype(BF)

        def one(step, carry):
            h = lax.bitwise_xor(s, step)
            pltpu.make_async_remote_copy(
                src_ref=gpack.at[h], dst_ref=glanded.at[s], send_sem=send3, recv_sem=recv3,
                device_id=(g, h), device_id_type=MESH,
            ).start()
            return carry

        lax.fori_loop(1, HEADS, one, 0)
        glanded[s] = gpack[s]

    def attend(j):
        wait_for(landed.at[j, pl.ds(1, GROUPS - 1)], recv2.at[j])
        for r in range(HEADS):
            m, z = (r % 2) * 4 + (r // 2) % 4, r // 8
            here = slice(r * TOK, (r + 1) * TOK)
            text = slice(VIDEO + r * TXT_DEV, VIDEO + (r + 1) * TXT_DEV)
            q_s[here, :] = landed[j, m, z, 0:TOK, :]
            k_s[here, :] = landed[j, m, z, TOK:2 * TOK, :]
            v_s[here, :] = landed[j, m, z, 2 * TOK:3 * TOK, :]
            k_s[text, :] = landed[j, m, z, 3 * TOK:3 * TOK + TXT_DEV, :]
            v_s[text, :] = landed[j, m, z, 3 * TOK + TXT_DEV:ROWS, :]
            g_s[here, :] = glanded[r, j]
        clip = source_group(dest_ref, g, j) * PLACES + j
        blocks = blocks_ref[clip]
        count = count_ref[clip]
        kt[...] = k_s[...].T
        vt[...] = v_s[...].T
        row = lax.broadcasted_iota(jnp.int32, (KEYS, HEAD), 0)
        dead = jnp.logical_or(
            jnp.logical_and(row >= blocks * BLK, row < VIDEO), row >= VIDEO + count
        )
        bias[...] = jnp.where(dead, NEG_FILL, 0.0)
        dk_s[...] = jnp.zeros_like(dk_s)
        dv_s[...] = jnp.zeros_like(dv_s)

        def one(i, carry):
            at = pl.ds(pl.multiple_of(i * BLK, BLK), BLK)
            q = q_s[at, :]
            gr = g_s[at, :]
            live = jnp.where(i < blocks, 1.0, 0.0).astype(F32)
            st = dot_nt(k_s[...], q) + jnp.concatenate([bias[...], bias[...]], axis=1)
            top = jnp.max(st, axis=0, keepdims=True)
            e = jnp.exp2((st - top) * (SCALE * LOG2E))
            w = e * (1.0 / jnp.sum(e, axis=0, keepdims=True))
            wb = w.astype(BF)
            o_s[j, at, :] = (dot_nn(vt[...], wb) * live).T.astype(BF)
            dv_s[...] += dot_nn(wb, gr)
            dp = dot_nt(v_s[...], gr)
            centre = jnp.sum(dp * w, axis=0, keepdims=True)
            ds = (w * (dp - centre) * SCALE).astype(BF)
            dq_s[at, :] = dot_nn(kt[...], ds).T.astype(BF)
            dk_s[...] += dot_nn(ds, q)
            return carry

        lax.fori_loop(0, VIDEO // BLK, one, 0)

        def send_att(step, carry):
            r = lax.bitwise_xor(s, step)
            pltpu.make_async_remote_copy(
                src_ref=o_s.at[j, token_rows(r), :], dst_ref=alanded.at[s, j],
                send_sem=asend.at[j], recv_sem=arecv.at[j], device_id=(g, r), device_id_type=MESH,
            ).start()
            return carry

        lax.fori_loop(1, HEADS, send_att, 0)
        alanded[s, j] = o_s[j, token_rows(s), :]
        spread_done(j)

        def send_back(step, carry):
            r = lax.bitwise_xor(s, step)
            pack[j, r, 0:TOK, :] = dq_s[token_rows(r), :]
            pack[j, r, TOK:2 * TOK, :] = dk_s[token_rows(r), :].astype(BF)
            pack[j, r, 2 * TOK:3 * TOK, :] = dv_s[token_rows(r), :].astype(BF)
            pack[j, r, 3 * TOK:3 * TOK + TXT_DEV, :] = dk_s[text_rows(r), :].astype(BF)
            pack[j, r, 3 * TOK + TXT_DEV:ROWS, :] = dv_s[text_rows(r), :].astype(BF)

            @pl.when(step > 0)
            def _():
                pltpu.make_async_remote_copy(
                    src_ref=pack.at[j, r], dst_ref=blanded.at[j, s],
                    send_sem=bsend.at[j], recv_sem=brecv.at[j],
                    device_id=(g, r), device_id_type=MESH,
                ).start()

            return carry

        lax.fori_loop(0, HEADS, send_back, 0)
        blanded[j, s] = pack[j, s]

    def forward(j):
        wait_for(alanded.at[pl.ds(1, HEADS - 1), j], arecv.at[j])

        def one(i, carry):
            pltpu.make_async_remote_copy(
                src_ref=alanded.at[2 * i + 1 - core, j], dst_ref=afwd.at[i, j],
                send_sem=fsend.at[j], recv_sem=frecv.at[j],
                device_id=(g, partner), device_id_type=MESH,
            ).start()
            return carry

        lax.fori_loop(0, HEADS // 2, one, 0)
        for h in range(HEADS):
            rows[j * TOK:(j + 1) * TOK, h * HEAD:(h + 1) * HEAD] = alanded[h, j]

    def collect(j):
        wait_for(blanded.at[j, pl.ds(1, HEADS - 1)], brecv.at[j])

        def one(h, carry):
            for t in range(3):
                gq_ref[j, :, head_columns(t, h)] = blanded[j, h, t * TOK:(t + 1) * TOK, :]
            for t in range(2):
                at = 3 * TOK + t * TXT_DEV
                gt_ref[j, :, head_columns(t, h)] = blanded[j, h, at:at + TXT_DEV, :]
            return carry

        lax.fori_loop(0, HEADS, one, 0)

    def term(pair, carry):
        mine = jnp.concatenate(
            [alanded[4 * pair + 2 * i + core].reshape(PLACES * TOK, HEAD) for i in range(2)], axis=1
        )
        theirs = jnp.concatenate(
            [afwd[2 * pair + i].reshape(PLACES * TOK, HEAD) for i in range(2)], axis=1
        )
        both = jnp.concatenate([mine, theirs], axis=0)
        for c in range(4):
            columns = slice(c * 768, (c + 1) * 768)
            right = jnp.concatenate(
                [out_ref[:, :, columns].reshape(PLACES * TOK, 768),
                 gpart[:, :, columns].reshape(PLACES * TOK, 768)], axis=0)
            value = dot_tn(both, right).astype(BF)
            for i in range(2):
                for b in range(2):
                    bits = cube_bits(2 * pair + i, jnp.int32(2 * c + b))
                    for p in range(PARTS):
                        rh, ct = p // 3, p % 3
                        top, left = i * HEAD + rh * 64, b * 384 + ct * HEAD
                        acc[p, cube_index(bits, ORDERS[p])] = value[
                            top:top + 64, left:left + HEAD
                        ]
        return carry

    own = cube_bits(s // 2, g)

    def exchange(p, k):
        dim = ORDERS[p][k]
        size = CHIPS // 2 >> k
        start = cube_index(own, ORDERS[p], k) + (1 - own[dim]) * size
        return pltpu.make_async_remote_copy(
            src_ref=acc.at[p, pl.ds(start, size)],
            dst_ref=arrived.at[p, pl.ds(CHIPS - 2 * size, size)],
            send_sem=rsend.at[p, k], recv_sem=rrecv.at[p, k],
            device_id=cube_neighbour(dim, g, s), device_id_type=MESH,
        )

    def reduce_stage(k):
        size = CHIPS // 2 >> k
        for p in range(PARTS):
            exchange(p, k).wait_recv()
            start = cube_index(own, ORDERS[p], k + 1)
            if k < 5:
                chunk = min(size, 4)

                def add(i, carry):
                    at = pl.ds(start + i * chunk, chunk)
                    come = pl.ds(CHIPS - 2 * size + i * chunk, chunk)
                    acc[p, at] = (acc[p, at].astype(F32) + arrived[p, come].astype(F32)).astype(BF)
                    return carry

                lax.fori_loop(0, size // chunk, add, 0)
                exchange(p, k + 1).start()
            else:
                rh, ct = p // 3, p % 3
                value = acc[p, start].astype(F32) + arrived[p, CHIPS - 2].astype(F32)
                gw_ref[rh * 64:(rh + 1) * 64, ct * HEAD:(ct + 1) * HEAD] = value * (
                    1.0 / (PLACES * GROUPS)
                )

    loads[PLACES].wait()
    spread(0)
    spread(1)
    loads[PLACES + 1].wait()
    lend = pltpu.make_async_remote_copy(
        src_ref=out_ref, dst_ref=gpart, send_sem=lend_send, recv_sem=lend_recv,
        device_id=(g, partner), device_id_type=MESH,
    )
    lend.start()
    project_grads()
    regroup(0)
    spread(2)
    regroup(1)
    spread(3)
    wait_for(glanded.at[pl.ds(1, HEADS - 1)], recv3)
    attend(0)
    regroup(2)
    attend(1)
    regroup(3)
    forward(0)
    attend(2)
    forward(1)
    attend(3)
    forward(2)
    collect(0)
    lend.wait()
    forward(3)
    for j in range(PLACES):
        wait_for(afwd.at[:, j], frecv.at[j])
    lax.fori_loop(0, 4, term, 0)
    for p in range(PARTS):
        exchange(p, 0).start()
    for c in range(D // COLUMNS):
        widen(c).wait()
        value = dot_nn(rows[...], wide[c % 2]).astype(BF)
        out_ref[:, :, c * COLUMNS:(c + 1) * COLUMNS] = value.reshape(PLACES, TOK, COLUMNS)
        if c + 2 < D // COLUMNS:
            widen(c + 2).start()
    collect(1)
    collect(2)
    for k in range(6):
        reduce_stage(k)
    collect(3)

    for j in range(PLACES):
        if j >= 2:
            wait_for(sorted_.at[j % 2, pl.ds(1, GROUPS - 1)], send2.at[j])
        wait_for(o_s.at[j, pl.ds(TOK, VIDEO - TOK)], asend.at[j])
        wait_for(afwd.at[:, j], fsend.at[j])
        wait_for(pack.at[j, pl.ds(1, HEADS - 1)], bsend.at[j])
    wait_for(gpack.at[pl.ds(1, HEADS - 1)], send3)
    for k in range(6):
        for p in range(PARTS):
            exchange(p, k).wait_send()


def on_device(qkv, text_kv, clip_blocks, text_count, dest_group, out_weight, grad_out):
    smem = pl.BlockSpec(memory_space=pltpu.SMEM)
    vmem = pl.BlockSpec(memory_space=pltpu.VMEM)
    hbm = pl.BlockSpec(memory_space=pl.ANY)
    dma = pltpu.SemaphoreType.DMA
    relay = pltpu.VMEM((GROUPS, 2, ROWS, HEAD), BF)
    return pl.pallas_call(
        kernel,
        out_shape=(
            jax.ShapeDtypeStruct((PLACES, TOK, D), BF),
            jax.ShapeDtypeStruct((PLACES, TOK, 3 * HW), BF),
            jax.ShapeDtypeStruct((PLACES, TXT_DEV, 2 * HW), BF),
            jax.ShapeDtypeStruct((HEAD, D // GROUPS), F32),
        ),
        in_specs=[smem] * 3 + [hbm] * 4,
        out_specs=(vmem,) * 4,
        scratch_shapes=[
            pltpu.VMEM((PLACES, HEADS, ROWS, HEAD), BF),
            relay, relay, relay, relay,
            pltpu.VMEM((2, GROUPS, 2, ROWS, HEAD), BF),
            pltpu.VMEM((PLACES, GROUPS, 2, ROWS, HEAD), BF),
            pltpu.VMEM((HEADS, PLACES, TOK, HEAD), BF),
            pltpu.VMEM((HEADS, PLACES, TOK, HEAD), BF),
            pltpu.VMEM((2, HW, COLUMNS), BF),
            pltpu.VMEM((PLACES * TOK, HW), F32),
            pltpu.VMEM((VIDEO, HEAD), BF),
            pltpu.VMEM((KEYS, HEAD), BF),
            pltpu.VMEM((KEYS, HEAD), BF),
            pltpu.VMEM((VIDEO, HEAD), BF),
            pltpu.VMEM((HEAD, KEYS), BF),
            pltpu.VMEM((HEAD, KEYS), BF),
            pltpu.VMEM((KEYS, HEAD), F32),
            pltpu.VMEM((PLACES, VIDEO, HEAD), BF),
            pltpu.VMEM((VIDEO, HEAD), BF),
            pltpu.VMEM((KEYS, HEAD), F32),
            pltpu.VMEM((KEYS, HEAD), F32),
            pltpu.VMEM((HEADS, PLACES, TOK, HEAD), BF),
            pltpu.VMEM((HEADS // 2, PLACES, TOK, HEAD), BF),
            pltpu.VMEM((PLACES, TOK, D), BF),
            pltpu.VMEM((PLACES, HEADS, ROWS, HEAD), BF),
            pltpu.VMEM((PARTS, CHIPS, 64, HEAD), BF),
            pltpu.VMEM((PARTS, CHIPS, 64, HEAD), BF),
            pltpu.VMEM((PLACES * TOK, HW), BF),
            dma((PLACES + 2,)), dma((2,)),
            dma((PLACES,)), dma((PLACES,)), dma((PLACES,)), dma((PLACES,)), dma, dma,
            dma((PLACES,)), dma((PLACES,)), dma((PLACES,)), dma((PLACES,)), dma, dma,
            dma((PLACES,)), dma((PLACES,)), dma((PARTS, 6)), dma((PARTS, 6)),
        ],
        compiler_params=pltpu.CompilerParams(
            collective_id=0, has_side_effects=True, vmem_limit_bytes=62 * 1024 * 1024
        ),
        name="video_attention",
    )(dest_group, clip_blocks, text_count, qkv, text_kv, grad_out, out_weight)


def solution(mesh):
    return jax.shard_map(
        on_device,
        mesh=mesh,
        in_specs=(
            P("grp", "seq", None),
            P("grp", "seq", None),
            P(),
            P(),
            P(),
            P(),
            P("grp", "seq", None),
        ),
        out_specs=(
            P("grp", "seq", None),
            P("grp", "seq", None),
            P("grp", "seq", None),
            P("seq", "grp"),
        ),
        check_vma=False,
    )
```

```python
import functools

import jax
import jax.numpy as jnp
from jax import lax
from jax.experimental import pallas as pl
from jax.experimental.pallas import tpu as pltpu
from jax.sharding import PartitionSpec as P

HEAD = 128
HEADS = 16
BLK = 256
GROUPS = 8
PLACES = 4
TOK = 64
TXT_DEV = 16
VIDEO = TOK * HEADS
TEXT = TXT_DEV * HEADS
KEYS = VIDEO + TEXT
HW = HEADS * HEAD
D = 3072
ROWS = 3 * TOK + 2 * TXT_DEV
SCALE = HEAD ** (-0.5)
LOG2E = 1.4426950408889634
NEG_FILL = -1e30
MESH = pl.DeviceIdType.MESH
BF = jnp.bfloat16
F32 = jnp.float32


def dot_nt(a, b):
    return lax.dot_general(a, b, (((1,), (1,)), ((), ())), preferred_element_type=F32)


def dot_nn(a, b):
    return lax.dot_general(a, b, (((1,), (0,)), ((), ())), preferred_element_type=F32)


def wait_for(ref, sem):
    pltpu.make_async_copy(ref, ref, sem).wait()


def source_group(dest_ref, group, place):
    found = jnp.int32(0)
    for g in range(GROUPS):
        found = jnp.where(dest_ref[g * PLACES + place] == group, g, found)
    return found


def group_at(z_lo, by_place, by_dest, parity):
    b1 = by_place + parity * (by_dest - by_place)
    b2 = by_dest + parity * (by_place - by_dest)
    return z_lo * 4 + b2 * 3 + (1 - 2 * b2) * b1


def enter():
    barrier = pltpu.get_barrier_semaphore()
    g, s = lax.axis_index("grp"), lax.axis_index("seq")
    me = g * HEADS + s

    def greet(step, carry):
        other = lax.rem(me + step, GROUPS * HEADS)
        pl.semaphore_signal(
            barrier, inc=1, device_id=(other // HEADS, lax.rem(other, HEADS)), device_id_type=MESH
        )
        return carry

    lax.fori_loop(1, GROUPS * HEADS, greet, 0)
    pl.semaphore_wait(barrier, GROUPS * HEADS - 1)


def dot_tn(a, b):
    return lax.dot_general(a, b, (((0,), (0,)), ((), ())), preferred_element_type=F32)


X1, X2, Y1, Y2, Z1, Z2 = range(6)
ORDERS = (
    (X1, Y1, Z1, X2, Y2, Z2),
    (Y1, Z1, X2, Y2, Z2, X1),
    (Z1, X2, Y2, Z2, X1, Y1),
    (X2, Y2, Z2, X1, Y1, Z1),
    (Y2, Z2, X1, Y1, Z1, X2),
    (Z2, X1, Y1, Z1, X2, Y2),
)
PARTS = 6
CHIPS = 64
COLUMNS = 512


def ring_bits(u):
    high = u // 2
    return lax.bitwise_xor(lax.rem(u, 2), high), high


def cube_bits(head_pair, column_block):
    x1, x2 = ring_bits(lax.rem(head_pair, 4))
    y1, y2 = ring_bits(lax.rem(column_block, 4))
    z1, z2 = ring_bits(2 * (head_pair // 4) + column_block // 4)
    return x1, x2, y1, y2, z1, z2


def cube_index(bits, order, count=6):
    at = jnp.int32(0)
    for k in range(count):
        at = at + bits[order[k]] * (CHIPS // 2 >> k)
    return at


def cube_neighbour(dim, g, s):
    z_lo, y = g // 4, lax.rem(g, 4)
    z_hi, x, core = s // 8, lax.rem(s // 2, 4), lax.rem(s, 2)
    if dim == X1:
        x = lax.bitwise_xor(x, 1)
    if dim == X2:
        x = 3 - x
    if dim == Y1:
        y = lax.bitwise_xor(y, 1)
    if dim == Y2:
        y = 3 - y
    if dim in (Z1, Z2):
        z_lo = 1 - z_lo
    if dim == Z2:
        z_hi = 1 - z_hi
    return z_lo * 4 + y, (z_hi * 4 + x) * 2 + core


def kernel(
    dest_ref, blocks_ref, count_ref, qkv_hbm, text_hbm, grad_hbm, weight_hbm,
    out_ref, gq_ref, gt_ref, gw_ref,
    pack, relay, sorted_, landed, gpack, glanded,
    wide, total, q_s, k_s, v_s, g_s, kt, vt, bias, o_s, dq_s, dk_s, dv_s,
    alanded, afwd, gpart, blanded, acc, arrived, rows,
    load_sem, wide_sem, send1, recv1, send2, recv2, send3, recv3,
    asend, arecv, fsend, frecv, lend_send, lend_recv, bsend, brecv, rsend, rrecv,
):
    g, s = lax.axis_index("grp"), lax.axis_index("seq")
    core = lax.rem(s, 2)
    partner = lax.bitwise_xor(s, 1)
    z_lo = g // 4
    ring = ring_bits(lax.rem(g, 4))

    def by_place(parity):
        return ring[0] + parity * (ring[1] - ring[0])

    def by_dest(parity):
        return ring[1] + parity * (ring[0] - ring[1])

    def place_of(parity):
        return 2 * z_lo + by_place(parity)

    place = place_of(core)
    mix = by_dest(core)
    home = mix == core
    away = jnp.logical_not(home)

    def unit_group(t, dest_bit):
        unit = lax.bitwise_xor(place, t)
        return group_at(unit // 2, lax.rem(unit, 2), dest_bit, core)

    def head_columns(t, h):
        return pl.ds(pl.multiple_of(t * HW + h * HEAD, HEAD), HEAD)

    def token_rows(r):
        return pl.ds(pl.multiple_of(r * TOK, TOK), TOK)

    def text_rows(r):
        return pl.ds(pl.multiple_of(VIDEO + r * TXT_DEV, TXT_DEV), TXT_DEV)

    loads = [pltpu.make_async_copy(qkv_hbm.at[j], gq_ref.at[j], load_sem.at[j]) for j in range(PLACES)]
    loads.append(pltpu.make_async_copy(text_hbm, gt_ref, load_sem.at[PLACES]))
    loads.append(pltpu.make_async_copy(grad_hbm, out_ref, load_sem.at[PLACES + 1]))

    def widen(c):
        return pltpu.make_async_copy(
            weight_hbm.at[:, c * COLUMNS:(c + 1) * COLUMNS], wide.at[c % 2], wide_sem.at[c % 2]
        )

    for load in loads:
        load.start()
    widen(0).start()
    widen(1).start()
    enter()

    def push(t, h):
        parity = lax.rem(h, 2)
        j = lax.bitwise_xor(place_of(parity), t)
        return pltpu.make_async_remote_copy(
            src_ref=pack.at[t, h], dst_ref=relay.at[g, s // 2],
            send_sem=send1.at[t], recv_sem=recv1,
            device_id=(group_at(j // 2, lax.rem(j, 2), core, parity), h), device_id_type=MESH,
        )

    def spread(t):
        def one(step, carry):
            h = lax.bitwise_xor(s, step)
            j = lax.bitwise_xor(place_of(lax.rem(h, 2)), t)
            for i in range(3):
                pack[t, h, i * TOK:(i + 1) * TOK, :] = gq_ref[j, :, head_columns(i, h)]
            for i in range(2):
                at = 3 * TOK + i * TXT_DEV
                pack[t, h, at:at + TXT_DEV, :] = gt_ref[j, :, head_columns(i, h)]

            @pl.when(jnp.logical_or(step + t > 0, away))
            def _():
                push(t, h).start()

            return carry

        lax.fori_loop(0, HEADS, one, 0)
        if t == 0:
            @pl.when(home)
            def _():
                pltpu.make_async_copy(pack.at[0, s], relay.at[g, s // 2], recv1).start()

    def spread_done(t):
        if t > 0:
            wait_for(pack.at[t], send1.at[t])
            return

        @pl.when(home)
        def _():
            wait_for(pack.at[0, pl.ds(1, HEADS - 1)], send1.at[0])

        @pl.when(away)
        def _():
            wait_for(pack.at[0], send1.at[0])

    def regroup():
        wait_for(relay, recv1)
        neighbour = group_at(z_lo, by_place(core), 1 - mix, core)
        for t in range(PLACES):
            sorted_[t] = relay[source_group(dest_ref, unit_group(t, 1 - mix), place)]
            pltpu.make_async_remote_copy(
                src_ref=sorted_.at[t], dst_ref=landed.at[t, mix],
                send_sem=send2, recv_sem=recv2.at[t],
                device_id=(neighbour, s), device_id_type=MESH,
            ).start()
        for t in range(PLACES):
            landed[t, mix] = relay[source_group(dest_ref, unit_group(t, mix), place)]

    def project_grads():
        for c in range(D // COLUMNS):
            widen(c).wait()
            part = dot_nt(
                out_ref[:, :, c * COLUMNS:(c + 1) * COLUMNS].reshape(PLACES * TOK, COLUMNS),
                wide[c % 2],
            )
            total[...] = part if c == 0 else total[...] + part
            widen((c + 2) % (D // COLUMNS)).start()
        for j in range(PLACES):
            blocks = blocks_ref[source_group(dest_ref, g, j) * PLACES + j]
            live = jnp.where(s // 4 < blocks, 1.0, 0.0).astype(F32)
            for h in range(HEADS):
                gpack[h, j] = (
                    total[j * TOK:(j + 1) * TOK, h * HEAD:(h + 1) * HEAD] * live
                ).astype(BF)

        for t in range(PLACES):
            def one(step, carry):
                h = lax.bitwise_xor(s, step)
                parity = lax.rem(h, 2)
                j = lax.bitwise_xor(place_of(parity), t)
                owner = group_at(j // 2, lax.rem(j, 2), by_dest(parity), parity)
                pltpu.make_async_remote_copy(
                    src_ref=gpack.at[h, j], dst_ref=glanded.at[t, s], send_sem=send3,
                    recv_sem=recv3.at[t], device_id=(owner, h), device_id_type=MESH,
                ).start()
                return carry

            lax.fori_loop(1 if t == 0 else 0, HEADS, one, 0)
        glanded[0, s] = gpack[s, place]

    def attend(t):
        low = 1 if t == 0 else 0
        wait_for(glanded.at[t, pl.ds(low, HEADS - low)], recv3.at[t])
        wait_for(sorted_.at[t], recv2.at[t])
        for r in range(HEADS):
            here = slice(r * TOK, (r + 1) * TOK)
            text = slice(VIDEO + r * TXT_DEV, VIDEO + (r + 1) * TXT_DEV)
            q_s[here, :] = landed[t, r % 2, r // 2, 0:TOK, :]
            k_s[here, :] = landed[t, r % 2, r // 2, TOK:2 * TOK, :]
            v_s[here, :] = landed[t, r % 2, r // 2, 2 * TOK:3 * TOK, :]
            k_s[text, :] = landed[t, r % 2, r // 2, 3 * TOK:3 * TOK + TXT_DEV, :]
            v_s[text, :] = landed[t, r % 2, r // 2, 3 * TOK + TXT_DEV:ROWS, :]
            g_s[here, :] = glanded[t, r]
        dest = unit_group(t, mix)
        clip = source_group(dest_ref, dest, place) * PLACES + place
        blocks = blocks_ref[clip]
        count = count_ref[clip]
        kt[...] = k_s[...].T
        vt[...] = v_s[...].T
        row = lax.broadcasted_iota(jnp.int32, (KEYS, HEAD), 0)
        dead = jnp.logical_or(
            jnp.logical_and(row >= blocks * BLK, row < VIDEO), row >= VIDEO + count
        )
        bias[...] = jnp.where(dead, NEG_FILL, 0.0)
        dk_s[...] = jnp.zeros_like(dk_s)
        dv_s[...] = jnp.zeros_like(dv_s)

        def one(i, carry):
            at = pl.ds(pl.multiple_of(i * BLK, BLK), BLK)
            q = q_s[at, :]
            gr = g_s[at, :]
            live = jnp.where(i < blocks, 1.0, 0.0).astype(F32)
            st = dot_nt(k_s[...], q) + jnp.concatenate([bias[...], bias[...]], axis=1)
            top = jnp.max(st, axis=0, keepdims=True)
            e = jnp.exp2((st - top) * (SCALE * LOG2E))
            w = e * (1.0 / jnp.sum(e, axis=0, keepdims=True))
            wb = w.astype(BF)
            o_s[t, at, :] = (dot_nn(vt[...], wb) * live).T.astype(BF)
            dv_s[...] += dot_nn(wb, gr)
            dp = dot_nt(v_s[...], gr)
            centre = jnp.sum(dp * w, axis=0, keepdims=True)
            ds = (w * (dp - centre) * SCALE).astype(BF)
            dq_s[at, :] = dot_nn(kt[...], ds).T.astype(BF)
            dk_s[...] += dot_nn(ds, q)
            return carry

        lax.fori_loop(0, VIDEO // BLK, one, 0)

        def send_att(step, carry):
            r = lax.bitwise_xor(s, step)
            pltpu.make_async_remote_copy(
                src_ref=o_s.at[t, token_rows(r), :], dst_ref=alanded.at[s, place],
                send_sem=asend.at[t], recv_sem=arecv.at[t],
                device_id=(dest, r), device_id_type=MESH,
            ).start()
            return carry

        lax.fori_loop(low, HEADS, send_att, 0)
        if t == 0:
            alanded[s, place] = o_s[t, token_rows(s), :]
        spread_done(t)

        def send_back(step, carry):
            r = lax.bitwise_xor(s, step)
            pack[t, r, 0:TOK, :] = dq_s[token_rows(r), :]
            pack[t, r, TOK:2 * TOK, :] = dk_s[token_rows(r), :].astype(BF)
            pack[t, r, 2 * TOK:3 * TOK, :] = dv_s[token_rows(r), :].astype(BF)
            pack[t, r, 3 * TOK:3 * TOK + TXT_DEV, :] = dk_s[text_rows(r), :].astype(BF)
            pack[t, r, 3 * TOK + TXT_DEV:ROWS, :] = dv_s[text_rows(r), :].astype(BF)

            @pl.when(step >= low)
            def _():
                pltpu.make_async_remote_copy(
                    src_ref=pack.at[t, r], dst_ref=blanded.at[t, s],
                    send_sem=bsend.at[t], recv_sem=brecv.at[t],
                    device_id=(dest, r), device_id_type=MESH,
                ).start()

            return carry

        lax.fori_loop(0, HEADS, send_back, 0)
        if t == 0:
            blanded[t, s] = pack[t, s]

    def forward(t):
        low = 1 if t == 0 else 0
        wait_for(alanded.at[pl.ds(low, HEADS - low), t], arecv.at[t])
        lent = lax.bitwise_xor(place_of(1 - core), t)

        def one(i, carry):
            pltpu.make_async_remote_copy(
                src_ref=alanded.at[2 * i + 1 - core, lent], dst_ref=afwd.at[i, lent],
                send_sem=fsend.at[t], recv_sem=frecv.at[t],
                device_id=(g, partner), device_id_type=MESH,
            ).start()
            return carry

        lax.fori_loop(0, HEADS // 2, one, 0)
        for h in range(HEADS):
            j = lax.bitwise_xor(place_of(h % 2), t)
            rows[token_rows(j), h * HEAD:(h + 1) * HEAD] = alanded[h, j]

    def collect(t):
        low = 1 if t == 0 else 0
        wait_for(blanded.at[t, pl.ds(low, HEADS - low)], brecv.at[t])

        def one(h, carry):
            j = lax.bitwise_xor(place_of(lax.rem(h, 2)), t)
            for i in range(3):
                gq_ref[j, :, head_columns(i, h)] = blanded[t, h, i * TOK:(i + 1) * TOK, :]
            for i in range(2):
                at = 3 * TOK + i * TXT_DEV
                gt_ref[j, :, head_columns(i, h)] = blanded[t, h, at:at + TXT_DEV, :]
            return carry

        lax.fori_loop(0, HEADS, one, 0)

    def term(pair, carry):
        mine = jnp.concatenate(
            [alanded[4 * pair + 2 * i + core].reshape(PLACES * TOK, HEAD) for i in range(2)], axis=1
        )
        theirs = jnp.concatenate(
            [afwd[2 * pair + i].reshape(PLACES * TOK, HEAD) for i in range(2)], axis=1
        )
        both = jnp.concatenate([mine, theirs], axis=0)
        for c in range(4):
            columns = slice(c * 768, (c + 1) * 768)
            right = jnp.concatenate(
                [out_ref[:, :, columns].reshape(PLACES * TOK, 768),
                 gpart[:, :, columns].reshape(PLACES * TOK, 768)], axis=0)
            value = dot_tn(both, right).astype(BF)
            for i in range(2):
                for b in range(2):
                    bits = cube_bits(2 * pair + i, jnp.int32(2 * c + b))
                    for p in range(PARTS):
                        rh, ct = p // 3, p % 3
                        top, left = i * HEAD + rh * 64, b * 384 + ct * HEAD
                        acc[p, cube_index(bits, ORDERS[p])] = value[
                            top:top + 64, left:left + HEAD
                        ]
        return carry

    own = cube_bits(s // 2, g)

    def exchange(p, k):
        dim = ORDERS[p][k]
        size = CHIPS // 2 >> k
        start = cube_index(own, ORDERS[p], k) + (1 - own[dim]) * size
        return pltpu.make_async_remote_copy(
            src_ref=acc.at[p, pl.ds(start, size)],
            dst_ref=arrived.at[p, pl.ds(CHIPS - 2 * size, size)],
            send_sem=rsend.at[p, k], recv_sem=rrecv.at[p, k],
            device_id=cube_neighbour(dim, g, s), device_id_type=MESH,
        )

    def reduce_stage(k):
        size = CHIPS // 2 >> k
        for p in range(PARTS):
            exchange(p, k).wait_recv()
            start = cube_index(own, ORDERS[p], k + 1)
            if k < 5:
                chunk = min(size, 4)

                def add(i, carry):
                    at = pl.ds(start + i * chunk, chunk)
                    come = pl.ds(CHIPS - 2 * size + i * chunk, chunk)
                    acc[p, at] = (acc[p, at].astype(F32) + arrived[p, come].astype(F32)).astype(BF)
                    return carry

                lax.fori_loop(0, size // chunk, add, 0)
                exchange(p, k + 1).start()
            else:
                rh, ct = p // 3, p % 3
                value = acc[p, start].astype(F32) + arrived[p, CHIPS - 2].astype(F32)
                gw_ref[rh * 64:(rh + 1) * 64, ct * HEAD:(ct + 1) * HEAD] = value * (
                    1.0 / (PLACES * GROUPS)
                )

    for load in loads[:PLACES + 1]:
        load.wait()
    for t in range(PLACES):
        spread(t)
    loads[PLACES + 1].wait()
    lend = pltpu.make_async_remote_copy(
        src_ref=out_ref, dst_ref=gpart, send_sem=lend_send, recv_sem=lend_recv,
        device_id=(g, partner), device_id_type=MESH,
    )
    lend.start()
    project_grads()
    regroup()
    attend(0)
    attend(1)
    forward(0)
    attend(2)
    forward(1)
    attend(3)
    forward(2)
    collect(0)
    lend.wait()
    forward(3)
    for j in range(PLACES):
        wait_for(afwd.at[:, j], frecv.at[j])
    lax.fori_loop(0, 4, term, 0)
    for p in range(PARTS):
        exchange(p, 0).start()
    for c in range(D // COLUMNS):
        widen(c).wait()
        value = dot_nn(rows[...], wide[c % 2]).astype(BF)
        out_ref[:, :, c * COLUMNS:(c + 1) * COLUMNS] = value.reshape(PLACES, TOK, COLUMNS)
        if c + 2 < D // COLUMNS:
            widen(c + 2).start()
    collect(1)
    collect(2)
    for k in range(6):
        reduce_stage(k)
    collect(3)

    for t in range(PLACES):
        low = 1 if t == 0 else 0
        wait_for(o_s.at[t, pl.ds(low * TOK, VIDEO - low * TOK)], asend.at[t])
        wait_for(afwd.at[:, t], fsend.at[t])
        wait_for(pack.at[t, pl.ds(low, HEADS - low)], bsend.at[t])
    wait_for(sorted_, send2)
    wait_for(gpack.at[:, pl.ds(1, PLACES - 1)], send3)
    wait_for(gpack.at[pl.ds(1, HEADS - 1), 0], send3)
    for k in range(6):
        for p in range(PARTS):
            exchange(p, k).wait_send()


def on_device(qkv, text_kv, clip_blocks, text_count, dest_group, out_weight, grad_out):
    smem = pl.BlockSpec(memory_space=pltpu.SMEM)
    vmem = pl.BlockSpec(memory_space=pltpu.VMEM)
    hbm = pl.BlockSpec(memory_space=pl.ANY)
    dma = pltpu.SemaphoreType.DMA
    return pl.pallas_call(
        kernel,
        out_shape=(
            jax.ShapeDtypeStruct((PLACES, TOK, D), BF),
            jax.ShapeDtypeStruct((PLACES, TOK, 3 * HW), BF),
            jax.ShapeDtypeStruct((PLACES, TXT_DEV, 2 * HW), BF),
            jax.ShapeDtypeStruct((HEAD, D // GROUPS), F32),
        ),
        in_specs=[smem] * 3 + [hbm] * 4,
        out_specs=(vmem,) * 4,
        scratch_shapes=[
            pltpu.VMEM((PLACES, HEADS, ROWS, HEAD), BF),
            pltpu.VMEM((GROUPS, HEADS // 2, ROWS, HEAD), BF),
            pltpu.VMEM((PLACES, HEADS // 2, ROWS, HEAD), BF),
            pltpu.VMEM((PLACES, 2, HEADS // 2, ROWS, HEAD), BF),
            pltpu.VMEM((HEADS, PLACES, TOK, HEAD), BF),
            pltpu.VMEM((PLACES, HEADS, TOK, HEAD), BF),
            pltpu.VMEM((2, HW, COLUMNS), BF),
            pltpu.VMEM((PLACES * TOK, HW), F32),
            pltpu.VMEM((VIDEO, HEAD), BF),
            pltpu.VMEM((KEYS, HEAD), BF),
            pltpu.VMEM((KEYS, HEAD), BF),
            pltpu.VMEM((VIDEO, HEAD), BF),
            pltpu.VMEM((HEAD, KEYS), BF),
            pltpu.VMEM((HEAD, KEYS), BF),
            pltpu.VMEM((KEYS, HEAD), F32),
            pltpu.VMEM((PLACES, VIDEO, HEAD), BF),
            pltpu.VMEM((VIDEO, HEAD), BF),
            pltpu.VMEM((KEYS, HEAD), F32),
            pltpu.VMEM((KEYS, HEAD), F32),
            pltpu.VMEM((HEADS, PLACES, TOK, HEAD), BF),
            pltpu.VMEM((HEADS // 2, PLACES, TOK, HEAD), BF),
            pltpu.VMEM((PLACES, TOK, D), BF),
            pltpu.VMEM((PLACES, HEADS, ROWS, HEAD), BF),
            pltpu.VMEM((PARTS, CHIPS, 64, HEAD), BF),
            pltpu.VMEM((PARTS, CHIPS, 64, HEAD), BF),
            pltpu.VMEM((PLACES * TOK, HW), BF),
            dma((PLACES + 2,)), dma((2,)),
            dma((PLACES,)), dma, dma, dma((PLACES,)), dma, dma((PLACES,)),
            dma((PLACES,)), dma((PLACES,)), dma((PLACES,)), dma((PLACES,)), dma, dma,
            dma((PLACES,)), dma((PLACES,)), dma((PARTS, 6)), dma((PARTS, 6)),
        ],
        compiler_params=pltpu.CompilerParams(
            collective_id=0, has_side_effects=True, vmem_limit_bytes=62 * 1024 * 1024
        ),
        name="video_attention",
    )(dest_group, clip_blocks, text_count, qkv, text_kv, grad_out, out_weight)


def solution(mesh):
    return jax.shard_map(
        on_device,
        mesh=mesh,
        in_specs=(
            P("grp", "seq", None),
            P("grp", "seq", None),
            P(),
            P(),
            P(),
            P(),
            P("grp", "seq", None),
        ),
        out_specs=(
            P("grp", "seq", None),
            P("grp", "seq", None),
            P("grp", "seq", None),
            P("seq", "grp"),
        ),
        check_vma=False,
    )
```

```python
import functools

import jax
import jax.numpy as jnp
from jax import lax
from jax.experimental import pallas as pl
from jax.experimental.pallas import tpu as pltpu
from jax.sharding import PartitionSpec as P

HEAD = 128
HEADS = 16
BLK = 256
GROUPS = 8
PLACES = 4
TOK = 64
TXT_DEV = 16
VIDEO = TOK * HEADS
TEXT = TXT_DEV * HEADS
KEYS = VIDEO + TEXT
HW = HEADS * HEAD
D = 3072
ROWS = 3 * TOK + 2 * TXT_DEV
SCALE = HEAD ** (-0.5)
LOG2E = 1.4426950408889634
NEG_FILL = -1e30
MESH = pl.DeviceIdType.MESH
BF = jnp.bfloat16
F32 = jnp.float32


def dot_nt(a, b):
    return lax.dot_general(a, b, (((1,), (1,)), ((), ())), preferred_element_type=F32)


def dot_nn(a, b):
    return lax.dot_general(a, b, (((1,), (0,)), ((), ())), preferred_element_type=F32)


def wait_for(ref, sem):
    pltpu.make_async_copy(ref, ref, sem).wait()


def source_group(dest_ref, group, place):
    found = jnp.int32(0)
    for g in range(GROUPS):
        found = jnp.where(dest_ref[g * PLACES + place] == group, g, found)
    return found


def group_at(z_lo, by_place, by_dest, parity):
    b1 = by_place + parity * (by_dest - by_place)
    b2 = by_dest + parity * (by_place - by_dest)
    return z_lo * 4 + b2 * 3 + (1 - 2 * b2) * b1


def enter():
    barrier = pltpu.get_barrier_semaphore()
    g, s = lax.axis_index("grp"), lax.axis_index("seq")
    me = g * HEADS + s

    def greet(step, carry):
        other = lax.rem(me + step, GROUPS * HEADS)
        pl.semaphore_signal(
            barrier, inc=1, device_id=(other // HEADS, lax.rem(other, HEADS)), device_id_type=MESH
        )
        return carry

    lax.fori_loop(1, GROUPS * HEADS, greet, 0)
    return barrier


def dot_tn(a, b):
    return lax.dot_general(a, b, (((0,), (0,)), ((), ())), preferred_element_type=F32)


X1, X2, Y1, Y2, Z1, Z2 = range(6)
ORDERS = (
    (X1, Y1, Z1, X2, Y2, Z2),
    (Y1, Z1, X2, Y2, Z2, X1),
    (Z1, X2, Y2, Z2, X1, Y1),
    (X2, Y2, Z2, X1, Y1, Z1),
    (Y2, Z2, X1, Y1, Z1, X2),
    (Z2, X1, Y1, Z1, X2, Y2),
)
PARTS = 6
CHIPS = 64
COLUMNS = 512
HALVINGS = 3


def ring_bits(u):
    high = u // 2
    return lax.bitwise_xor(lax.rem(u, 2), high), high


def cube_bits(head_pair, column_block):
    x1, x2 = ring_bits(lax.rem(head_pair, 4))
    y1, y2 = ring_bits(lax.rem(column_block, 4))
    z1, z2 = ring_bits(2 * (head_pair // 4) + column_block // 4)
    return x1, x2, y1, y2, z1, z2


def cube_index(bits, order, count=6):
    at = jnp.int32(0)
    for k in range(count):
        at = at + bits[order[k]] * (CHIPS // 2 >> k)
    return at


def cube_neighbour(dims, g, s):
    across = {X1: (1, 0, 0), X2: (3, 0, 0), Y1: (0, 1, 0), Y2: (0, 3, 0), Z1: (0, 0, 1), Z2: (0, 0, 3)}
    x = lax.rem(s // 2, 4)
    y = lax.rem(g, 4)
    z = 2 * (s // 8) + g // 4
    for dim in dims:
        dx, dy, dz = across[dim]
        x = lax.bitwise_xor(x, dx) if dx else x
        y = lax.bitwise_xor(y, dy) if dy else y
        z = lax.bitwise_xor(z, dz) if dz else z
    return lax.rem(z, 2) * 4 + y, ((z // 2) * 4 + x) * 2 + lax.rem(s, 2)


def kernel(
    dest_ref, blocks_ref, count_ref, qkv_hbm, text_hbm, grad_hbm, weight_hbm,
    out_ref, gq_ref, gt_ref, gw_ref,
    pack, relay, sorted_, landed, gpack, glanded,
    wide, total, q_s, k_s, v_s, g_s, turned, bias, stats, st_s, dp_s, wb_s, ds_s, o_s, dq_s, dk_s, dv_s,
    alanded, afwd, gpart, blanded, acc, arrived, rows,
    load_sem, wide_sem, send1, recv1, send2, recv2, send3, recv3,
    asend, arecv, fsend, frecv, lend_send, lend_recv, bsend, brecv, rsend, rrecv,
):
    g, s = lax.axis_index("grp"), lax.axis_index("seq")
    core = lax.rem(s, 2)
    partner = lax.bitwise_xor(s, 1)
    z_lo = g // 4
    ring = ring_bits(lax.rem(g, 4))

    def by_place(parity):
        return ring[0] + parity * (ring[1] - ring[0])

    def by_dest(parity):
        return ring[1] + parity * (ring[0] - ring[1])

    def place_of(parity):
        return 2 * z_lo + by_place(parity)

    place = place_of(core)
    mix = by_dest(core)
    home = mix == core
    away = jnp.logical_not(home)

    def unit_group(t, dest_bit):
        unit = lax.bitwise_xor(place, t)
        return group_at(unit // 2, lax.rem(unit, 2), dest_bit, core)

    def head_columns(t, h):
        return pl.ds(pl.multiple_of(t * HW + h * HEAD, HEAD), HEAD)

    def token_rows(r):
        return pl.ds(pl.multiple_of(r * TOK, TOK), TOK)

    def text_rows(r):
        return pl.ds(pl.multiple_of(VIDEO + r * TXT_DEV, TXT_DEV), TXT_DEV)

    loads = [pltpu.make_async_copy(qkv_hbm.at[j], gq_ref.at[j], load_sem.at[j]) for j in range(PLACES)]
    loads.append(pltpu.make_async_copy(text_hbm, gt_ref, load_sem.at[PLACES]))
    loads.append(pltpu.make_async_copy(grad_hbm, out_ref, load_sem.at[PLACES + 1]))

    def widen(c):
        return pltpu.make_async_copy(
            weight_hbm.at[:, c * COLUMNS:(c + 1) * COLUMNS], wide.at[c % 2], wide_sem.at[c % 2]
        )

    for load in loads:
        load.start()
    widen(0).start()
    widen(1).start()
    barrier = enter()

    def push(t, h):
        parity = lax.rem(h, 2)
        j = lax.bitwise_xor(place_of(parity), t)
        return pltpu.make_async_remote_copy(
            src_ref=pack.at[t, h], dst_ref=relay.at[g, s // 2],
            send_sem=send1.at[t], recv_sem=recv1,
            device_id=(group_at(j // 2, lax.rem(j, 2), core, parity), h), device_id_type=MESH,
        )

    def fill(t):
        def one(h, carry):
            j = lax.bitwise_xor(place_of(lax.rem(h, 2)), t)
            for i in range(3):
                pack[t, h, i * TOK:(i + 1) * TOK, :] = gq_ref[j, :, head_columns(i, h)]
            for i in range(2):
                at = 3 * TOK + i * TXT_DEV
                pack[t, h, at:at + TXT_DEV, :] = gt_ref[j, :, head_columns(i, h)]
            return carry

        lax.fori_loop(0, HEADS, one, 0)

    def spread(t):
        def one(step, carry):
            push(t, lax.bitwise_xor(s, step)).start()
            return carry

        lax.fori_loop(1 if t == 0 else 0, HEADS, one, 0)
        if t == 0:
            @pl.when(away)
            def _():
                push(0, s).start()

            @pl.when(home)
            def _():
                pltpu.make_async_copy(pack.at[0, s], relay.at[g, s // 2], recv1).start()

    def spread_done(t):
        if t > 0:
            wait_for(pack.at[t], send1.at[t])
            return

        @pl.when(home)
        def _():
            wait_for(pack.at[0, pl.ds(1, HEADS - 1)], send1.at[0])

        @pl.when(away)
        def _():
            wait_for(pack.at[0], send1.at[0])

    def regroup(t):
        neighbour = group_at(z_lo, by_place(core), 1 - mix, core)
        sorted_[t] = relay[source_group(dest_ref, unit_group(t, 1 - mix), place)]
        pltpu.make_async_remote_copy(
            src_ref=sorted_.at[t], dst_ref=landed.at[t, mix],
            send_sem=send2, recv_sem=recv2.at[t],
            device_id=(neighbour, s), device_id_type=MESH,
        ).start()
        landed[t, mix] = relay[source_group(dest_ref, unit_group(t, mix), place)]

    def project_grads():
        for c in range(D // COLUMNS):
            widen(c).wait()
            part = dot_nt(
                out_ref[:, :, c * COLUMNS:(c + 1) * COLUMNS].reshape(PLACES * TOK, COLUMNS),
                wide[c % 2],
            )
            total[...] = part if c == 0 else total[...] + part
            widen((c + 2) % (D // COLUMNS)).start()
        for j in range(PLACES):
            blocks = blocks_ref[source_group(dest_ref, g, j) * PLACES + j]
            live = jnp.where(s // 4 < blocks, 1.0, 0.0).astype(F32)
            for h in range(HEADS):
                gpack[h, j] = (
                    total[j * TOK:(j + 1) * TOK, h * HEAD:(h + 1) * HEAD] * live
                ).astype(BF)

    def send_grads(t):
        def one(step, carry):
            h = lax.bitwise_xor(s, step)
            parity = lax.rem(h, 2)
            j = lax.bitwise_xor(place_of(parity), t)
            owner = group_at(j // 2, lax.rem(j, 2), by_dest(parity), parity)
            pltpu.make_async_remote_copy(
                src_ref=gpack.at[h, j], dst_ref=glanded.at[t, s], send_sem=send3,
                recv_sem=recv3.at[t], device_id=(owner, h), device_id_type=MESH,
            ).start()
            return carry

        lax.fori_loop(1 if t == 0 else 0, HEADS, one, 0)
        if t == 0:
            glanded[0, s] = gpack[s, place]

    def gather(t, back):
        low = 1 if t == 0 else 0
        if not back:
            wait_for(sorted_.at[t], recv2.at[t])
        for r in range(HEADS):
            here = slice(r * TOK, (r + 1) * TOK)
            text = slice(VIDEO + r * TXT_DEV, VIDEO + (r + 1) * TXT_DEV)
            q_s[here, :] = landed[t, r % 2, r // 2, 0:TOK, :]
            k_s[here, :] = landed[t, r % 2, r // 2, TOK:2 * TOK, :]
            v_s[here, :] = landed[t, r % 2, r // 2, 2 * TOK:3 * TOK, :]
            k_s[text, :] = landed[t, r % 2, r // 2, 3 * TOK:3 * TOK + TXT_DEV, :]
            v_s[text, :] = landed[t, r % 2, r // 2, 3 * TOK + TXT_DEV:ROWS, :]
        clip = source_group(dest_ref, unit_group(t, mix), place) * PLACES + place
        turned[...] = k_s[...].T if back else v_s[...].T
        row = lax.broadcasted_iota(jnp.int32, (KEYS, HEAD), 0)
        dead = jnp.logical_or(
            jnp.logical_and(row >= blocks_ref[clip] * BLK, row < VIDEO),
            row >= VIDEO + count_ref[clip],
        )
        bias[...] = jnp.where(dead, NEG_FILL, 0.0)
        if back:
            wait_for(glanded.at[t, pl.ds(low, HEADS - low)], recv3.at[t])
            for r in range(HEADS):
                g_s[r * TOK:(r + 1) * TOK, :] = glanded[t, r]

    def queries(i):
        return slice(i * BLK, (i + 1) * BLK)

    def score(i):
        st = dot_nt(k_s[...], q_s[queries(i), :])
        st = st + jnp.concatenate([bias[...], bias[...]], axis=1)
        st_s[i % 2] = st
        return st

    def attend(t):
        blocks = blocks_ref[source_group(dest_ref, unit_group(t, mix), place) * PLACES + place]
        count = VIDEO // BLK

        def top_of(st):
            return jnp.max(st.reshape(KEYS // 8, 8, BLK), axis=0)

        top = top_of(score(0))
        for i in range(count):
            n = i % 2
            peak = jnp.max(top, axis=0, keepdims=True)
            if i + 1 < count:
                top = top_of(score(i + 1))
            part = jnp.zeros((8, BLK), F32)
            for c in range(KEYS // TOK):
                r = slice(c * TOK, (c + 1) * TOK)
                e = jnp.exp2((st_s[n, r, :] - peak) * (SCALE * LOG2E))
                st_s[n, r, :] = e
                part = part + jnp.sum(e.reshape(TOK // 8, 8, BLK), axis=0)
            share = 1.0 / jnp.sum(part, axis=0, keepdims=True)
            stats[t, i, 0:1, :] = peak
            stats[t, i, 1:2, :] = share
            for c in range(KEYS // TOK):
                r = slice(c * TOK, (c + 1) * TOK)
                wb_s[n, r, :] = (st_s[n, r, :] * share).astype(BF)
            live = jnp.where(i < blocks, 1.0, 0.0).astype(F32)
            o_s[t, queries(i), :] = (dot_nn(turned[...], wb_s[n]) * live).T.astype(BF)

    def attend_back(t):
        count = VIDEO // BLK

        def mixing(i):
            dp_s[i % 2] = dot_nt(v_s[...], g_s[queries(i), :])

        def add_keys(i):
            n = i % 2
            term = dot_nn(ds_s[n], q_s[queries(i), :])
            dk_s[...] = term if i == 0 else dk_s[...] + term
            dq_s[queries(i), :] = (dot_nn(turned[...], ds_s[n]) * SCALE).T.astype(BF)

        score(0)
        mixing(0)
        for i in range(count):
            n = i % 2
            if i + 1 < count:
                score(i + 1)
            peak, share = stats[t, i, 0:1, :], stats[t, i, 1:2, :]
            part = jnp.zeros((8, BLK), F32)
            for c in range(KEYS // TOK):
                r = slice(c * TOK, (c + 1) * TOK)
                w = jnp.exp2((st_s[n, r, :] - peak) * (SCALE * LOG2E)) * share
                st_s[n, r, :] = w
                wb_s[n, r, :] = w.astype(BF)
                part = part + jnp.sum((w * dp_s[n, r, :]).reshape(TOK // 8, 8, BLK), axis=0)
            if i > 0:
                add_keys(i - 1)
            if i + 1 < count:
                mixing(i + 1)
            term = dot_nn(wb_s[n], g_s[queries(i), :])
            dv_s[...] = term if i == 0 else dv_s[...] + term
            centre = jnp.sum(part, axis=0, keepdims=True)
            for c in range(KEYS // TOK):
                r = slice(c * TOK, (c + 1) * TOK)
                ds_s[n, r, :] = (st_s[n, r, :] * (dp_s[n, r, :] - centre)).astype(BF)
        add_keys(count - 1)
        pack_back(t)
        send_back(t)

    def send_att(t):
        dest = unit_group(t, mix)

        def one(step, carry):
            r = lax.bitwise_xor(s, step)
            pltpu.make_async_remote_copy(
                src_ref=o_s.at[t, token_rows(r), :], dst_ref=alanded.at[s, place],
                send_sem=asend.at[t], recv_sem=arecv.at[t],
                device_id=(dest, r), device_id_type=MESH,
            ).start()
            return carry

        lax.fori_loop(1 if t == 0 else 0, HEADS, one, 0)
        if t == 0:
            alanded[s, place] = o_s[t, token_rows(s), :]

    def pack_back(t):
        spread_done(t)

        def one(r, carry):
            pack[t, r, 0:TOK, :] = dq_s[token_rows(r), :]
            pack[t, r, TOK:2 * TOK, :] = (dk_s[token_rows(r), :] * SCALE).astype(BF)
            pack[t, r, 2 * TOK:3 * TOK, :] = dv_s[token_rows(r), :].astype(BF)
            at = 3 * TOK
            pack[t, r, at:at + TXT_DEV, :] = (dk_s[text_rows(r), :] * SCALE).astype(BF)
            pack[t, r, at + TXT_DEV:ROWS, :] = dv_s[text_rows(r), :].astype(BF)
            return carry

        lax.fori_loop(0, HEADS, one, 0)
        if t == 0:
            blanded[t, s] = pack[t, s]

    def send_back(t):
        dest = unit_group(t, mix)

        def one(step, carry):
            r = lax.bitwise_xor(s, step)
            pltpu.make_async_remote_copy(
                src_ref=pack.at[t, r], dst_ref=blanded.at[t, s],
                send_sem=bsend.at[t], recv_sem=brecv.at[t],
                device_id=(dest, r), device_id_type=MESH,
            ).start()
            return carry

        lax.fori_loop(1 if t == 0 else 0, HEADS, one, 0)

    def forward(t):
        low = 1 if t == 0 else 0
        wait_for(alanded.at[pl.ds(low, HEADS - low), t], arecv.at[t])
        lent = lax.bitwise_xor(place_of(1 - core), t)

        def one(i, carry):
            pltpu.make_async_remote_copy(
                src_ref=alanded.at[2 * i + 1 - core, lent], dst_ref=afwd.at[i, lent],
                send_sem=fsend.at[t], recv_sem=frecv.at[t],
                device_id=(g, partner), device_id_type=MESH,
            ).start()
            return carry

        lax.fori_loop(0, HEADS // 2, one, 0)
        for h in range(HEADS):
            j = lax.bitwise_xor(place_of(h % 2), t)
            rows[token_rows(j), h * HEAD:(h + 1) * HEAD] = alanded[h, j]

    def collect(t):
        low = 1 if t == 0 else 0
        wait_for(blanded.at[t, pl.ds(low, HEADS - low)], brecv.at[t])

        def one(h, carry):
            j = lax.bitwise_xor(place_of(lax.rem(h, 2)), t)
            for i in range(3):
                gq_ref[j, :, head_columns(i, h)] = blanded[t, h, i * TOK:(i + 1) * TOK, :]
            for i in range(2):
                at = 3 * TOK + i * TXT_DEV
                gt_ref[j, :, head_columns(i, h)] = blanded[t, h, at:at + TXT_DEV, :]
            return carry

        lax.fori_loop(0, HEADS, one, 0)

    def term(pair, carry):
        mine = jnp.concatenate(
            [alanded[4 * pair + 2 * i + core].reshape(PLACES * TOK, HEAD) for i in range(2)], axis=1
        )
        theirs = jnp.concatenate(
            [afwd[2 * pair + i].reshape(PLACES * TOK, HEAD) for i in range(2)], axis=1
        )
        both = jnp.concatenate([mine, theirs], axis=0)
        for c in range(4):
            columns = slice(c * 768, (c + 1) * 768)
            right = jnp.concatenate(
                [out_ref[:, :, columns].reshape(PLACES * TOK, 768),
                 gpart[:, :, columns].reshape(PLACES * TOK, 768)], axis=0)
            value = dot_tn(both, right).astype(BF)
            for i in range(2):
                for b in range(2):
                    bits = cube_bits(2 * pair + i, jnp.int32(2 * c + b))
                    for p in range(PARTS):
                        rh, ct = p // 3, p % 3
                        top, left = i * HEAD + rh * 64, b * 384 + ct * HEAD
                        acc[p, cube_index(bits, ORDERS[p])] = value[
                            top:top + 64, left:left + HEAD
                        ]
        return carry

    own = cube_bits(s // 2, g)

    def exchange(p, k):
        dim = ORDERS[p][k]
        size = CHIPS // 2 >> k
        start = cube_index(own, ORDERS[p], k) + (1 - own[dim]) * size
        return pltpu.make_async_remote_copy(
            src_ref=acc.at[p, pl.ds(start, size)],
            dst_ref=arrived.at[p, pl.ds(CHIPS - 2 * size, size)],
            send_sem=rsend.at[p, k], recv_sem=rrecv.at[p, k],
            device_id=cube_neighbour((dim,), g, s), device_id_type=MESH,
        )

    def deal(p, step):
        dims = ORDERS[p][HALVINGS:]
        at = cube_index(own, ORDERS[p], HALVINGS)
        for k, dim in enumerate(dims):
            bit = 4 >> k
            at = at + (1 - own[dim] if step & bit else own[dim]) * bit
        return pltpu.make_async_remote_copy(
            src_ref=acc.at[p, at], dst_ref=arrived.at[p, CHIPS - 8 + step],
            send_sem=rsend.at[p, HALVINGS], recv_sem=rrecv.at[p, HALVINGS],
            device_id=cube_neighbour([d for k, d in enumerate(dims) if step & (4 >> k)], g, s),
            device_id_type=MESH,
        )

    def reduce_stage(k):
        size = CHIPS // 2 >> k
        for p in range(PARTS):
            exchange(p, k).wait_recv()
            start = cube_index(own, ORDERS[p], k + 1)

            def add(i, carry):
                at = pl.ds(start + i * 4, 4)
                come = pl.ds(CHIPS - 2 * size + i * 4, 4)
                acc[p, at] = (acc[p, at].astype(F32) + arrived[p, come].astype(F32)).astype(BF)
                return carry

            lax.fori_loop(0, size // 4, add, 0)
            if k < HALVINGS - 1:
                exchange(p, k + 1).start()
            else:
                for step in range(1, 8):
                    deal(p, step).start()

    def reduce_last():
        for p in range(PARTS):
            wait_for(arrived.at[p, pl.ds(CHIPS - 7, 7)], rrecv.at[p, HALVINGS])
            value = acc[p, cube_index(own, ORDERS[p])].astype(F32)
            for step in range(1, 8):
                value = value + arrived[p, CHIPS - 8 + step].astype(F32)
            rh, ct = p // 3, p % 3
            gw_ref[rh * 64:(rh + 1) * 64, ct * HEAD:(ct + 1) * HEAD] = value * (
                1.0 / (PLACES * GROUPS)
            )

    def project_out():
        for c in range(D // COLUMNS):
            widen(c).wait()
            value = dot_nn(rows[...], wide[c % 2]).astype(BF)
            out_ref[:, :, c * COLUMNS:(c + 1) * COLUMNS] = value.reshape(PLACES, TOK, COLUMNS)
            if c + 2 < D // COLUMNS:
                widen(c + 2).start()

    for load in loads[:PLACES + 1]:
        load.wait()
    for t in range(PLACES):
        fill(t)
    pl.semaphore_wait(barrier, GROUPS * HEADS - 1)
    for t in range(PLACES):
        spread(t)
    loads[PLACES + 1].wait()
    project_grads()
    wait_for(relay, recv1)
    for t in range(2):
        regroup(t)
        send_grads(t)
    lend = pltpu.make_async_remote_copy(
        src_ref=out_ref, dst_ref=gpart, send_sem=lend_send, recv_sem=lend_recv,
        device_id=(g, partner), device_id_type=MESH,
    )
    lend.start()
    for t in range(PLACES):
        gather(t, False)
        if t == 0:
            for later in range(2, PLACES):
                regroup(later)
                send_grads(later)
        attend(t)
        send_att(t)
        if t == 0:
            gather(0, True)
            attend_back(0)
    gather(1, True)
    attend_back(1)
    for t in range(PLACES):
        forward(t)
    lend.wait()
    for t in range(PLACES):
        wait_for(afwd.at[:, t], frecv.at[t])
    lax.fori_loop(0, 4, term, 0)
    for p in range(PARTS):
        exchange(p, 0).start()
    gather(2, True)
    attend_back(2)
    reduce_stage(0)
    gather(3, True)
    attend_back(3)
    reduce_stage(1)
    project_out()
    collect(0)
    reduce_stage(2)
    collect(1)
    collect(2)
    reduce_last()
    collect(3)

    for t in range(PLACES):
        low = 1 if t == 0 else 0
        wait_for(o_s.at[t, pl.ds(low * TOK, VIDEO - low * TOK)], asend.at[t])
        wait_for(afwd.at[:, t], fsend.at[t])
        wait_for(pack.at[t, pl.ds(low, HEADS - low)], bsend.at[t])
    wait_for(sorted_, send2)
    wait_for(gpack.at[:, pl.ds(1, PLACES - 1)], send3)
    wait_for(gpack.at[pl.ds(1, HEADS - 1), 0], send3)
    for p in range(PARTS):
        for k in range(HALVINGS):
            exchange(p, k).wait_send()
        wait_for(arrived.at[p, pl.ds(CHIPS - 7, 7)], rsend.at[p, HALVINGS])


def on_device(qkv, text_kv, clip_blocks, text_count, dest_group, out_weight, grad_out):
    smem = pl.BlockSpec(memory_space=pltpu.SMEM)
    vmem = pl.BlockSpec(memory_space=pltpu.VMEM)
    hbm = pl.BlockSpec(memory_space=pl.ANY)
    dma = pltpu.SemaphoreType.DMA
    return pl.pallas_call(
        kernel,
        out_shape=(
            jax.ShapeDtypeStruct((PLACES, TOK, D), BF),
            jax.ShapeDtypeStruct((PLACES, TOK, 3 * HW), BF),
            jax.ShapeDtypeStruct((PLACES, TXT_DEV, 2 * HW), BF),
            jax.ShapeDtypeStruct((HEAD, D // GROUPS), F32),
        ),
        in_specs=[smem] * 3 + [hbm] * 4,
        out_specs=(vmem,) * 4,
        scratch_shapes=[
            pltpu.VMEM((PLACES, HEADS, ROWS, HEAD), BF),
            pltpu.VMEM((GROUPS, HEADS // 2, ROWS, HEAD), BF),
            pltpu.VMEM((PLACES, HEADS // 2, ROWS, HEAD), BF),
            pltpu.VMEM((PLACES, 2, HEADS // 2, ROWS, HEAD), BF),
            pltpu.VMEM((HEADS, PLACES, TOK, HEAD), BF),
            pltpu.VMEM((PLACES, HEADS, TOK, HEAD), BF),
            pltpu.VMEM((2, HW, COLUMNS), BF),
            pltpu.VMEM((PLACES * TOK, HW), F32),
            pltpu.VMEM((VIDEO, HEAD), BF),
            pltpu.VMEM((KEYS, HEAD), BF),
            pltpu.VMEM((KEYS, HEAD), BF),
            pltpu.VMEM((VIDEO, HEAD), BF),
            pltpu.VMEM((HEAD, KEYS), BF),
            pltpu.VMEM((KEYS, HEAD), F32),
            pltpu.VMEM((PLACES, VIDEO // BLK, 8, BLK), F32),
            pltpu.VMEM((2, KEYS, BLK), F32),
            pltpu.VMEM((2, KEYS, BLK), F32),
            pltpu.VMEM((2, KEYS, BLK), BF),
            pltpu.VMEM((2, KEYS, BLK), BF),
            pltpu.VMEM((PLACES, VIDEO, HEAD), BF),
            pltpu.VMEM((VIDEO, HEAD), BF),
            pltpu.VMEM((KEYS, HEAD), F32),
            pltpu.VMEM((KEYS, HEAD), F32),
            pltpu.VMEM((HEADS, PLACES, TOK, HEAD), BF),
            pltpu.VMEM((HEADS // 2, PLACES, TOK, HEAD), BF),
            pltpu.VMEM((PLACES, TOK, D), BF),
            pltpu.VMEM((PLACES, HEADS, ROWS, HEAD), BF),
            pltpu.VMEM((PARTS, CHIPS, 64, HEAD), BF),
            pltpu.VMEM((PARTS, CHIPS, 64, HEAD), BF),
            pltpu.VMEM((PLACES * TOK, HW), BF),
            dma((PLACES + 2,)), dma((2,)),
            dma((PLACES,)), dma, dma, dma((PLACES,)), dma, dma((PLACES,)),
            dma((PLACES,)), dma((PLACES,)), dma((PLACES,)), dma((PLACES,)), dma, dma,
            dma((PLACES,)), dma((PLACES,)), dma((PARTS, HALVINGS + 1)), dma((PARTS, HALVINGS + 1)),
        ],
        compiler_params=pltpu.CompilerParams(
            collective_id=0, has_side_effects=True, vmem_limit_bytes=62 * 1024 * 1024
        ),
        name="video_attention",
    )(dest_group, clip_blocks, text_count, qkv, text_kv, grad_out, out_weight)


def solution(mesh):
    return jax.shard_map(
        on_device,
        mesh=mesh,
        in_specs=(
            P("grp", "seq", None),
            P("grp", "seq", None),
            P(),
            P(),
            P(),
            P(),
            P("grp", "seq", None),
        ),
        out_specs=(
            P("grp", "seq", None),
            P("grp", "seq", None),
            P("grp", "seq", None),
            P("seq", "grp"),
        ),
        check_vma=False,
    )
```

```python
import functools

import jax
import jax.numpy as jnp
from jax import lax
from jax.experimental import pallas as pl
from jax.experimental.pallas import tpu as pltpu
from jax.sharding import PartitionSpec as P

HEAD = 128
HEADS = 16
BLK = 256
GROUPS = 8
PLACES = 4
TOK = 64
TXT_DEV = 16
VIDEO = TOK * HEADS
TEXT = TXT_DEV * HEADS
KEYS = VIDEO + TEXT
HW = HEADS * HEAD
D = 3072
ROWS = 3 * TOK + 2 * TXT_DEV
SCALE = HEAD ** (-0.5)
LOG2E = 1.4426950408889634
NEG_FILL = -1e30
MESH = pl.DeviceIdType.MESH
BF = jnp.bfloat16
F32 = jnp.float32


def dot_nt(a, b):
    return lax.dot_general(a, b, (((1,), (1,)), ((), ())), preferred_element_type=F32)


def dot_nn(a, b):
    return lax.dot_general(a, b, (((1,), (0,)), ((), ())), preferred_element_type=F32)


def wait_for(ref, sem):
    pltpu.make_async_copy(ref, ref, sem).wait()


def source_group(dest_ref, group, place):
    found = jnp.int32(0)
    for g in range(GROUPS):
        found = jnp.where(dest_ref[g * PLACES + place] == group, g, found)
    return found


def group_at(z_lo, by_place, by_dest, parity):
    b1 = by_place + parity * (by_dest - by_place)
    b2 = by_dest + parity * (by_place - by_dest)
    return z_lo * 4 + b2 * 3 + (1 - 2 * b2) * b1


def enter():
    barrier = pltpu.get_barrier_semaphore()
    g, s = lax.axis_index("grp"), lax.axis_index("seq")
    me = g * HEADS + s

    def greet(step, carry):
        other = lax.rem(me + step, GROUPS * HEADS)
        pl.semaphore_signal(
            barrier, inc=1, device_id=(other // HEADS, lax.rem(other, HEADS)), device_id_type=MESH
        )
        return carry

    lax.fori_loop(1, GROUPS * HEADS, greet, 0)
    return barrier


def dot_tn(a, b):
    return lax.dot_general(a, b, (((0,), (0,)), ((), ())), preferred_element_type=F32)


X1, X2, Y1, Y2, Z1, Z2 = range(6)
ORDERS = (
    (X1, Y1, Z1, X2, Y2, Z2),
    (Y1, Z1, X2, Y2, Z2, X1),
    (Z1, X2, Y2, Z2, X1, Y1),
    (X2, Y2, Z2, X1, Y1, Z1),
    (Y2, Z2, X1, Y1, Z1, X2),
    (Z2, X1, Y1, Z1, X2, Y2),
)
PARTS = 6
CHIPS = 64
COLUMNS = 512
HALVINGS = 3


def ring_bits(u):
    high = u // 2
    return lax.bitwise_xor(lax.rem(u, 2), high), high


def cube_bits(head_pair, column_block):
    x1, x2 = ring_bits(lax.rem(head_pair, 4))
    y1, y2 = ring_bits(lax.rem(column_block, 4))
    z1, z2 = ring_bits(2 * (head_pair // 4) + column_block // 4)
    return x1, x2, y1, y2, z1, z2


def cube_index(bits, order, count=6):
    at = jnp.int32(0)
    for k in range(count):
        at = at + bits[order[k]] * (CHIPS // 2 >> k)
    return at


def cube_neighbour(dims, g, s):
    across = {X1: (1, 0, 0), X2: (3, 0, 0), Y1: (0, 1, 0), Y2: (0, 3, 0), Z1: (0, 0, 1), Z2: (0, 0, 3)}
    x = lax.rem(s // 2, 4)
    y = lax.rem(g, 4)
    z = 2 * (s // 8) + g // 4
    for dim in dims:
        dx, dy, dz = across[dim]
        x = lax.bitwise_xor(x, dx) if dx else x
        y = lax.bitwise_xor(y, dy) if dy else y
        z = lax.bitwise_xor(z, dz) if dz else z
    return lax.rem(z, 2) * 4 + y, ((z // 2) * 4 + x) * 2 + lax.rem(s, 2)


def kernel(
    dest_ref, blocks_ref, count_ref, qkv_hbm, text_hbm, grad_hbm, weight_hbm,
    out_ref, gq_ref, gt_ref, gw_ref,
    pack, relay, sorted_, landed, gpack, glanded,
    wide, total, q_s, k_s, v_s, g_s, turned, bias, stats, st_s, dp_s, wb_s, ds_s, o_s, dq_s, dk_s, dv_s,
    alanded, afwd, gpart, blanded, acc, arrived, rows,
    load_sem, wide_sem, send1, recv1, send2, recv2, send3, recv3,
    asend, arecv, fsend, frecv, lend_send, lend_recv, bsend, brecv, rsend, rrecv,
):
    g, s = lax.axis_index("grp"), lax.axis_index("seq")
    core = lax.rem(s, 2)
    partner = lax.bitwise_xor(s, 1)
    z_lo = g // 4
    ring = ring_bits(lax.rem(g, 4))

    def by_place(parity):
        return ring[0] + parity * (ring[1] - ring[0])

    def by_dest(parity):
        return ring[1] + parity * (ring[0] - ring[1])

    def place_of(parity):
        return 2 * z_lo + by_place(parity)

    place = place_of(core)
    mix = by_dest(core)
    home = mix == core
    away = jnp.logical_not(home)

    def unit_group(t, dest_bit):
        unit = lax.bitwise_xor(place, t)
        return group_at(unit // 2, lax.rem(unit, 2), dest_bit, core)

    def head_columns(t, h):
        return pl.ds(pl.multiple_of(t * HW + h * HEAD, HEAD), HEAD)

    def token_rows(r):
        return pl.ds(pl.multiple_of(r * TOK, TOK), TOK)

    def text_rows(r):
        return pl.ds(pl.multiple_of(VIDEO + r * TXT_DEV, TXT_DEV), TXT_DEV)

    loads = [pltpu.make_async_copy(qkv_hbm.at[j], gq_ref.at[j], load_sem.at[j]) for j in range(PLACES)]
    loads.append(pltpu.make_async_copy(text_hbm, gt_ref, load_sem.at[PLACES]))
    loads.append(pltpu.make_async_copy(grad_hbm, out_ref, load_sem.at[PLACES + 1]))

    def widen(c):
        return pltpu.make_async_copy(
            weight_hbm.at[:, c * COLUMNS:(c + 1) * COLUMNS], wide.at[c % 2], wide_sem.at[c % 2]
        )

    for load in loads:
        load.start()
    widen(0).start()
    widen(1).start()
    barrier = enter()

    def push(t, h):
        parity = lax.rem(h, 2)
        j = lax.bitwise_xor(place_of(parity), t)
        return pltpu.make_async_remote_copy(
            src_ref=pack.at[t, h], dst_ref=relay.at[g, s // 2],
            send_sem=send1.at[t], recv_sem=recv1,
            device_id=(group_at(j // 2, lax.rem(j, 2), core, parity), h), device_id_type=MESH,
        )

    def fill(t):
        def one(h, carry):
            j = lax.bitwise_xor(place_of(lax.rem(h, 2)), t)
            for i in range(3):
                pack[t, h, i * TOK:(i + 1) * TOK, :] = gq_ref[j, :, head_columns(i, h)]
            for i in range(2):
                at = 3 * TOK + i * TXT_DEV
                pack[t, h, at:at + TXT_DEV, :] = gt_ref[j, :, head_columns(i, h)]
            return carry

        lax.fori_loop(0, HEADS, one, 0)

    def spread(t):
        def one(step, carry):
            push(t, lax.bitwise_xor(s, step)).start()
            return carry

        lax.fori_loop(1 if t == 0 else 0, HEADS, one, 0)
        if t == 0:
            @pl.when(away)
            def _():
                push(0, s).start()

            @pl.when(home)
            def _():
                pltpu.make_async_copy(pack.at[0, s], relay.at[g, s // 2], recv1).start()

    def spread_done(t, low):
        if not low:
            wait_for(pack.at[t], send1.at[t])
            return

        @pl.when(home)
        def _():
            wait_for(pack.at[0, pl.ds(1, HEADS - 1)], send1.at[0])

        @pl.when(away)
        def _():
            wait_for(pack.at[0], send1.at[0])

    def regroup(t):
        neighbour = group_at(z_lo, by_place(core), 1 - mix, core)
        sorted_[t] = relay[source_group(dest_ref, unit_group(t, 1 - mix), place)]
        pltpu.make_async_remote_copy(
            src_ref=sorted_.at[t], dst_ref=landed.at[t, mix],
            send_sem=send2, recv_sem=recv2.at[t],
            device_id=(neighbour, s), device_id_type=MESH,
        ).start()
        landed[t, mix] = relay[source_group(dest_ref, unit_group(t, mix), place)]

    def project_grads():
        for c in range(D // COLUMNS):
            widen(c).wait()
            part = dot_nt(
                out_ref[:, :, c * COLUMNS:(c + 1) * COLUMNS].reshape(PLACES * TOK, COLUMNS),
                wide[c % 2],
            )
            total[...] = part if c == 0 else total[...] + part
            widen((c + 2) % (D // COLUMNS)).start()
        for j in range(PLACES):
            blocks = blocks_ref[source_group(dest_ref, g, j) * PLACES + j]
            live = jnp.where(s // 4 < blocks, 1.0, 0.0).astype(F32)
            for h in range(HEADS):
                gpack[h, j] = (
                    total[j * TOK:(j + 1) * TOK, h * HEAD:(h + 1) * HEAD] * live
                ).astype(BF)

    def send_grads(t):
        def one(step, carry):
            h = lax.bitwise_xor(s, step)
            parity = lax.rem(h, 2)
            j = lax.bitwise_xor(place_of(parity), t)
            owner = group_at(j // 2, lax.rem(j, 2), by_dest(parity), parity)
            pltpu.make_async_remote_copy(
                src_ref=gpack.at[h, j], dst_ref=glanded.at[t, s], send_sem=send3,
                recv_sem=recv3.at[t], device_id=(owner, h), device_id_type=MESH,
            ).start()
            return carry

        lax.fori_loop(1 if t == 0 else 0, HEADS, one, 0)
        if t == 0:
            glanded[0, s] = gpack[s, place]

    def gather(t, back, low=0):
        if not back:
            wait_for(sorted_.at[t], recv2.at[t])
        for r in range(HEADS):
            here = slice(r * TOK, (r + 1) * TOK)
            text = slice(VIDEO + r * TXT_DEV, VIDEO + (r + 1) * TXT_DEV)
            q_s[here, :] = landed[t, r % 2, r // 2, 0:TOK, :]
            k_s[here, :] = landed[t, r % 2, r // 2, TOK:2 * TOK, :]
            v_s[here, :] = landed[t, r % 2, r // 2, 2 * TOK:3 * TOK, :]
            k_s[text, :] = landed[t, r % 2, r // 2, 3 * TOK:3 * TOK + TXT_DEV, :]
            v_s[text, :] = landed[t, r % 2, r // 2, 3 * TOK + TXT_DEV:ROWS, :]
        clip = source_group(dest_ref, unit_group(t, mix), place) * PLACES + place
        turned[...] = k_s[...].T if back else v_s[...].T
        row = lax.broadcasted_iota(jnp.int32, (KEYS, HEAD), 0)
        dead = jnp.logical_or(
            jnp.logical_and(row >= blocks_ref[clip] * BLK, row < VIDEO),
            row >= VIDEO + count_ref[clip],
        )
        bias[...] = jnp.where(dead, NEG_FILL, 0.0)
        if back:
            wait_for(glanded.at[t, pl.ds(low, HEADS - low)], recv3.at[t])
            for r in range(HEADS):
                g_s[r * TOK:(r + 1) * TOK, :] = glanded[t, r]

    def queries(i):
        return slice(i * BLK, (i + 1) * BLK)

    def score(i):
        st = dot_nt(k_s[...], q_s[queries(i), :])
        st = st + jnp.concatenate([bias[...], bias[...]], axis=1)
        st_s[i % 2] = st
        return st

    def attend(t):
        blocks = blocks_ref[source_group(dest_ref, unit_group(t, mix), place) * PLACES + place]
        count = VIDEO // BLK

        def top_of(st):
            return jnp.max(st.reshape(KEYS // 8, 8, BLK), axis=0)

        top = top_of(score(0))
        for i in range(count):
            n = i % 2
            peak = jnp.max(top, axis=0, keepdims=True)
            if i + 1 < count:
                top = top_of(score(i + 1))
            part = jnp.zeros((8, BLK), F32)
            for c in range(KEYS // TOK):
                r = slice(c * TOK, (c + 1) * TOK)
                e = jnp.exp2((st_s[n, r, :] - peak) * (SCALE * LOG2E))
                st_s[n, r, :] = e
                part = part + jnp.sum(e.reshape(TOK // 8, 8, BLK), axis=0)
            share = 1.0 / jnp.sum(part, axis=0, keepdims=True)
            stats[t, i, 0:1, :] = peak
            stats[t, i, 1:2, :] = share
            for c in range(KEYS // TOK):
                r = slice(c * TOK, (c + 1) * TOK)
                wb_s[n, r, :] = (st_s[n, r, :] * share).astype(BF)
            live = jnp.where(i < blocks, 1.0, 0.0).astype(F32)
            o_s[t, queries(i), :] = (dot_nn(turned[...], wb_s[n]) * live).T.astype(BF)

    def attend_back(t, low=0):
        count = VIDEO // BLK

        def mixing(i):
            dp_s[i % 2] = dot_nt(v_s[...], g_s[queries(i), :])

        def add_keys(i):
            n = i % 2
            term = dot_nn(ds_s[n], q_s[queries(i), :])
            dk_s[...] = term if i == 0 else dk_s[...] + term
            dq_s[queries(i), :] = (dot_nn(turned[...], ds_s[n]) * SCALE).T.astype(BF)

        score(0)
        mixing(0)
        for i in range(count):
            n = i % 2
            if i + 1 < count:
                score(i + 1)
            peak, share = stats[t, i, 0:1, :], stats[t, i, 1:2, :]
            part = jnp.zeros((8, BLK), F32)
            for c in range(KEYS // TOK):
                r = slice(c * TOK, (c + 1) * TOK)
                w = jnp.exp2((st_s[n, r, :] - peak) * (SCALE * LOG2E)) * share
                st_s[n, r, :] = w
                wb_s[n, r, :] = w.astype(BF)
                part = part + jnp.sum((w * dp_s[n, r, :]).reshape(TOK // 8, 8, BLK), axis=0)
            if i > 0:
                add_keys(i - 1)
            if i + 1 < count:
                mixing(i + 1)
            term = dot_nn(wb_s[n], g_s[queries(i), :])
            dv_s[...] = term if i == 0 else dv_s[...] + term
            centre = jnp.sum(part, axis=0, keepdims=True)
            for c in range(KEYS // TOK):
                r = slice(c * TOK, (c + 1) * TOK)
                ds_s[n, r, :] = (st_s[n, r, :] * (dp_s[n, r, :] - centre)).astype(BF)
        add_keys(count - 1)
        pack_back(t, low)
        send_back(t, low)

    def send_att(t, low=0):
        dest = unit_group(t, mix)

        def one(step, carry):
            r = lax.bitwise_xor(s, step)
            pltpu.make_async_remote_copy(
                src_ref=o_s.at[t, token_rows(r), :], dst_ref=alanded.at[s, place],
                send_sem=asend.at[t], recv_sem=arecv.at[t],
                device_id=(dest, r), device_id_type=MESH,
            ).start()
            return carry

        lax.fori_loop(low, HEADS, one, 0)
        if low:
            alanded[s, place] = o_s[t, token_rows(s), :]

    def pack_back(t, low):
        spread_done(t, low)

        def one(r, carry):
            pack[t, r, 0:TOK, :] = dq_s[token_rows(r), :]
            pack[t, r, TOK:2 * TOK, :] = (dk_s[token_rows(r), :] * SCALE).astype(BF)
            pack[t, r, 2 * TOK:3 * TOK, :] = dv_s[token_rows(r), :].astype(BF)
            at = 3 * TOK
            pack[t, r, at:at + TXT_DEV, :] = (dk_s[text_rows(r), :] * SCALE).astype(BF)
            pack[t, r, at + TXT_DEV:ROWS, :] = dv_s[text_rows(r), :].astype(BF)
            return carry

        lax.fori_loop(0, HEADS, one, 0)
        if low:
            blanded[t, s] = pack[t, s]

    def send_back(t, low):
        dest = unit_group(t, mix)

        def one(step, carry):
            r = lax.bitwise_xor(s, step)
            pltpu.make_async_remote_copy(
                src_ref=pack.at[t, r], dst_ref=blanded.at[t, s],
                send_sem=bsend.at[t], recv_sem=brecv.at[t],
                device_id=(dest, r), device_id_type=MESH,
            ).start()
            return carry

        lax.fori_loop(low, HEADS, one, 0)

    def forward(t):
        low = 1 if t == 0 else 0
        wait_for(alanded.at[pl.ds(low, HEADS - low), t], arecv.at[t])
        lent = lax.bitwise_xor(place_of(1 - core), t)

        def one(i, carry):
            pltpu.make_async_remote_copy(
                src_ref=alanded.at[2 * i + 1 - core, lent], dst_ref=afwd.at[i, lent],
                send_sem=fsend.at[t], recv_sem=frecv.at[t],
                device_id=(g, partner), device_id_type=MESH,
            ).start()
            return carry

        lax.fori_loop(0, HEADS // 2, one, 0)
        for h in range(HEADS):
            j = lax.bitwise_xor(place_of(h % 2), t)
            rows[token_rows(j), h * HEAD:(h + 1) * HEAD] = alanded[h, j]

    def collect(t):
        low = 1 if t == 0 else 0
        wait_for(blanded.at[t, pl.ds(low, HEADS - low)], brecv.at[t])

        def one(h, carry):
            j = lax.bitwise_xor(place_of(lax.rem(h, 2)), t)
            for i in range(3):
                gq_ref[j, :, head_columns(i, h)] = blanded[t, h, i * TOK:(i + 1) * TOK, :]
            for i in range(2):
                at = 3 * TOK + i * TXT_DEV
                gt_ref[j, :, head_columns(i, h)] = blanded[t, h, at:at + TXT_DEV, :]
            return carry

        lax.fori_loop(0, HEADS, one, 0)

    def term(pair, carry):
        mine = jnp.concatenate(
            [alanded[4 * pair + 2 * i + core].reshape(PLACES * TOK, HEAD) for i in range(2)], axis=1
        )
        theirs = jnp.concatenate(
            [afwd[2 * pair + i].reshape(PLACES * TOK, HEAD) for i in range(2)], axis=1
        )
        both = jnp.concatenate([mine, theirs], axis=0)
        for c in range(4):
            columns = slice(c * 768, (c + 1) * 768)
            right = jnp.concatenate(
                [out_ref[:, :, columns].reshape(PLACES * TOK, 768),
                 gpart[:, :, columns].reshape(PLACES * TOK, 768)], axis=0)
            value = dot_tn(both, right).astype(BF)
            for i in range(2):
                for b in range(2):
                    bits = cube_bits(2 * pair + i, jnp.int32(2 * c + b))
                    for p in range(PARTS):
                        rh, ct = p // 3, p % 3
                        top, left = i * HEAD + rh * 64, b * 384 + ct * HEAD
                        acc[p, cube_index(bits, ORDERS[p])] = value[
                            top:top + 64, left:left + HEAD
                        ]
        return carry

    own = cube_bits(s // 2, g)

    def exchange(p, k):
        dim = ORDERS[p][k]
        size = CHIPS // 2 >> k
        start = cube_index(own, ORDERS[p], k) + (1 - own[dim]) * size
        return pltpu.make_async_remote_copy(
            src_ref=acc.at[p, pl.ds(start, size)],
            dst_ref=arrived.at[p, pl.ds(CHIPS - 2 * size, size)],
            send_sem=rsend.at[p, k], recv_sem=rrecv.at[p, k],
            device_id=cube_neighbour((dim,), g, s), device_id_type=MESH,
        )

    def deal(p, step):
        dims = ORDERS[p][HALVINGS:]
        at = cube_index(own, ORDERS[p], HALVINGS)
        for k, dim in enumerate(dims):
            bit = 4 >> k
            at = at + (1 - own[dim] if step & bit else own[dim]) * bit
        return pltpu.make_async_remote_copy(
            src_ref=acc.at[p, at], dst_ref=arrived.at[p, CHIPS - 8 + step],
            send_sem=rsend.at[p, HALVINGS], recv_sem=rrecv.at[p, HALVINGS],
            device_id=cube_neighbour([d for k, d in enumerate(dims) if step & (4 >> k)], g, s),
            device_id_type=MESH,
        )

    def reduce_stage(k):
        size = CHIPS // 2 >> k
        for p in range(PARTS):
            exchange(p, k).wait_recv()
            start = cube_index(own, ORDERS[p], k + 1)

            def add(i, carry):
                at = pl.ds(start + i * 4, 4)
                come = pl.ds(CHIPS - 2 * size + i * 4, 4)
                acc[p, at] = (acc[p, at].astype(F32) + arrived[p, come].astype(F32)).astype(BF)
                return carry

            lax.fori_loop(0, size // 4, add, 0)
            if k < HALVINGS - 1:
                exchange(p, k + 1).start()
            else:
                for step in range(1, 8):
                    deal(p, step).start()

    def reduce_last():
        for p in range(PARTS):
            wait_for(arrived.at[p, pl.ds(CHIPS - 7, 7)], rrecv.at[p, HALVINGS])
            value = acc[p, cube_index(own, ORDERS[p])].astype(F32)
            for step in range(1, 8):
                value = value + arrived[p, CHIPS - 8 + step].astype(F32)
            rh, ct = p // 3, p % 3
            gw_ref[rh * 64:(rh + 1) * 64, ct * HEAD:(ct + 1) * HEAD] = value * (
                1.0 / (PLACES * GROUPS)
            )

    def project_out():
        for c in range(D // COLUMNS):
            widen(c).wait()
            value = dot_nn(rows[...], wide[c % 2]).astype(BF)
            out_ref[:, :, c * COLUMNS:(c + 1) * COLUMNS] = value.reshape(PLACES, TOK, COLUMNS)
            if c + 2 < D // COLUMNS:
                widen(c + 2).start()

    for load in loads[:PLACES + 1]:
        load.wait()
    for t in range(PLACES):
        fill(t)
    pl.semaphore_wait(barrier, GROUPS * HEADS - 1)
    for t in range(PLACES):
        spread(t)
    loads[PLACES + 1].wait()
    project_grads()
    wait_for(relay, recv1)
    for t in range(2):
        regroup(t)
        send_grads(t)
    lend = pltpu.make_async_remote_copy(
        src_ref=out_ref, dst_ref=gpart, send_sem=lend_send, recv_sem=lend_recv,
        device_id=(g, partner), device_id_type=MESH,
    )
    lend.start()
    gather(0, False)
    for later in range(2, PLACES):
        regroup(later)
        send_grads(later)
    attend(0)
    send_att(0, 1)
    gather(0, True, 1)
    attend_back(0, 1)

    def onward(t, carry):
        gather(t, False)
        attend(t)
        send_att(t)
        return carry

    def backward(t, carry):
        gather(t, True)
        attend_back(t)
        return carry

    lax.fori_loop(1, PLACES, onward, 0)
    backward(1, 0)
    for t in range(PLACES):
        forward(t)
    lend.wait()
    for t in range(PLACES):
        wait_for(afwd.at[:, t], frecv.at[t])
    lax.fori_loop(0, 4, term, 0)
    for p in range(PARTS):
        exchange(p, 0).start()
    lax.fori_loop(2, PLACES, backward, 0)
    reduce_stage(0)
    reduce_stage(1)
    project_out()
    collect(0)
    reduce_stage(2)
    collect(1)
    collect(2)
    reduce_last()
    collect(3)

    for t in range(PLACES):
        low = 1 if t == 0 else 0
        wait_for(o_s.at[t, pl.ds(low * TOK, VIDEO - low * TOK)], asend.at[t])
        wait_for(afwd.at[:, t], fsend.at[t])
        wait_for(pack.at[t, pl.ds(low, HEADS - low)], bsend.at[t])
    wait_for(sorted_, send2)
    wait_for(gpack.at[:, pl.ds(1, PLACES - 1)], send3)
    wait_for(gpack.at[pl.ds(1, HEADS - 1), 0], send3)
    for p in range(PARTS):
        for k in range(HALVINGS):
            exchange(p, k).wait_send()
        wait_for(arrived.at[p, pl.ds(CHIPS - 7, 7)], rsend.at[p, HALVINGS])


def on_device(qkv, text_kv, clip_blocks, text_count, dest_group, out_weight, grad_out):
    smem = pl.BlockSpec(memory_space=pltpu.SMEM)
    vmem = pl.BlockSpec(memory_space=pltpu.VMEM)
    hbm = pl.BlockSpec(memory_space=pl.ANY)
    dma = pltpu.SemaphoreType.DMA
    return pl.pallas_call(
        kernel,
        out_shape=(
            jax.ShapeDtypeStruct((PLACES, TOK, D), BF),
            jax.ShapeDtypeStruct((PLACES, TOK, 3 * HW), BF),
            jax.ShapeDtypeStruct((PLACES, TXT_DEV, 2 * HW), BF),
            jax.ShapeDtypeStruct((HEAD, D // GROUPS), F32),
        ),
        in_specs=[smem] * 3 + [hbm] * 4,
        out_specs=(vmem,) * 4,
        scratch_shapes=[
            pltpu.VMEM((PLACES, HEADS, ROWS, HEAD), BF),
            pltpu.VMEM((GROUPS, HEADS // 2, ROWS, HEAD), BF),
            pltpu.VMEM((PLACES, HEADS // 2, ROWS, HEAD), BF),
            pltpu.VMEM((PLACES, 2, HEADS // 2, ROWS, HEAD), BF),
            pltpu.VMEM((HEADS, PLACES, TOK, HEAD), BF),
            pltpu.VMEM((PLACES, HEADS, TOK, HEAD), BF),
            pltpu.VMEM((2, HW, COLUMNS), BF),
            pltpu.VMEM((PLACES * TOK, HW), F32),
            pltpu.VMEM((VIDEO, HEAD), BF),
            pltpu.VMEM((KEYS, HEAD), BF),
            pltpu.VMEM((KEYS, HEAD), BF),
            pltpu.VMEM((VIDEO, HEAD), BF),
            pltpu.VMEM((HEAD, KEYS), BF),
            pltpu.VMEM((KEYS, HEAD), F32),
            pltpu.VMEM((PLACES, VIDEO // BLK, 8, BLK), F32),
            pltpu.VMEM((2, KEYS, BLK), F32),
            pltpu.VMEM((2, KEYS, BLK), F32),
            pltpu.VMEM((2, KEYS, BLK), BF),
            pltpu.VMEM((2, KEYS, BLK), BF),
            pltpu.VMEM((PLACES, VIDEO, HEAD), BF),
            pltpu.VMEM((VIDEO, HEAD), BF),
            pltpu.VMEM((KEYS, HEAD), F32),
            pltpu.VMEM((KEYS, HEAD), F32),
            pltpu.VMEM((HEADS, PLACES, TOK, HEAD), BF),
            pltpu.VMEM((HEADS // 2, PLACES, TOK, HEAD), BF),
            pltpu.VMEM((PLACES, TOK, D), BF),
            pltpu.VMEM((PLACES, HEADS, ROWS, HEAD), BF),
            pltpu.VMEM((PARTS, CHIPS, 64, HEAD), BF),
            pltpu.VMEM((PARTS, CHIPS, 64, HEAD), BF),
            pltpu.VMEM((PLACES * TOK, HW), BF),
            dma((PLACES + 2,)), dma((2,)),
            dma((PLACES,)), dma, dma, dma((PLACES,)), dma, dma((PLACES,)),
            dma((PLACES,)), dma((PLACES,)), dma((PLACES,)), dma((PLACES,)), dma, dma,
            dma((PLACES,)), dma((PLACES,)), dma((PARTS, HALVINGS + 1)), dma((PARTS, HALVINGS + 1)),
        ],
        compiler_params=pltpu.CompilerParams(
            collective_id=0, has_side_effects=True, vmem_limit_bytes=62 * 1024 * 1024
        ),
        name="video_attention",
    )(dest_group, clip_blocks, text_count, qkv, text_kv, grad_out, out_weight)


def solution(mesh):
    return jax.shard_map(
        on_device,
        mesh=mesh,
        in_specs=(
            P("grp", "seq", None),
            P("grp", "seq", None),
            P(),
            P(),
            P(),
            P(),
            P("grp", "seq", None),
        ),
        out_specs=(
            P("grp", "seq", None),
            P("grp", "seq", None),
            P("grp", "seq", None),
            P("seq", "grp"),
        ),
        check_vma=False,
    )
```
